512 devices in a mesh: dp: 8 (over z_hi, x), tensor: 64 (over z_lo, y, core).
Axes of the slice: x: 4, y: 4, z: 16 (z_hi: 2, z_lo: 8; z = z_hi * 8 + z_lo), core: 2. Of those that a mesh axis runs over, the one named last changes fastest.
Arguments:
- tokens: bfloat16 [4096, 8192], P('dp', 'tensor'), may hold values from -6 to 6
- cotangent: bfloat16 [4096, 8192], P('dp', 'tensor'), may hold values from -6 to 6
- up_first: bfloat16 [64, 256, 128], P('tensor'), may hold values from -0.5 to 0.5
- up_second: bfloat16 [256, 64, 128], P('tensor'), may hold values from -0.75 to 0.75
- down_first: bfloat16 [256, 64, 128], P('tensor'), may hold values from -0.5 to 0.5
- down_second: bfloat16 [64, 256, 128], P('tensor'), may hold values from -0.375 to 0.375
Outputs:
- layer_out: bfloat16 [4096, 8192], P('dp', 'tensor')
- grad_tokens: bfloat16 [4096, 8192], P('dp', 'tensor')
- grad_up_first: float32 [64, 256, 128], P('tensor', 'dp')
- grad_up_second: float32 [256, 64, 128], P('tensor', 'dp')
- grad_down_first: float32 [256, 64, 128], P('tensor', 'dp')
- grad_down_second: float32 [64, 256, 128], P('tensor', 'dp')
The draws below stay inside these ranges and needn't reach their ends.
All inputs are finite; a program needn't handle non-finite values.
Results may differ from the reference program's by a relative error of at most 0.0061.
Values may be sent and summed in bfloat16 or wider, within the bound.
A program may use at most 64 MiB of HBM per device.

```python
import jax
import jax.numpy as jnp
from jax import lax

D = 8192
BLK = 128
DB = 64
HK = 256
TOKENS = 4096


def levels(rng, shape, pieces, least, top_value):
    def one(position, parts):
        draws = jax.random.uniform(jax.random.fold_in(jax.random.fold_in(rng, 6), position), (parts,), jnp.float32, least / len(pieces), top_value / len(pieces))
        return jnp.repeat(jnp.exp(draws), shape[position] // parts).reshape((-1,) + (1,) * (len(shape) - position - 1))

    factor_of = one(*pieces[0])
    for cut in pieces[1:]:
        factor_of = factor_of * one(*cut)
    return factor_of


def gaussian(rng, shape, scale, bound, pieces=(), held_as=jnp.bfloat16):
    result = scale * jax.random.normal(rng, shape, jnp.float32)
    if pieces:
        result = result * levels(rng, shape, pieces, -0.22, 0.18)
    return jnp.clip(result, -bound, bound).astype(held_as)


def setup_inputs(seed: int = 0) -> dict:
    key_of = jax.random.split(jax.random.key(seed), 7)
    return {
        "tokens": gaussian(key_of[0], (TOKENS, D), 1.0, 6.0, ((0, 8), (1, 64))),
        "cotangent": gaussian(key_of[1], (TOKENS, D), 1.0, 6.0, ((0, 8), (1, 64))),
        "up_first": gaussian(key_of[2], (DB, HK, BLK), BLK ** -0.5, 0.5, ((0, 64),)),
        "up_second": gaussian(key_of[3], (HK, DB, BLK), DB ** -0.5, 0.75, ((0, 64),)),
        "down_first": gaussian(key_of[4], (HK, DB, BLK), BLK ** -0.5, 0.5, ((0, 64),)),
        "down_second": gaussian(key_of[5], (DB, HK, BLK), HK ** -0.5, 0.375, ((0, 64),)),
    }


def rounded(value):
    return lax.optimization_barrier(value.astype(jnp.bfloat16)).astype(jnp.float32)


def silu_slope(preact):
    sigma = jax.nn.sigmoid(preact)
    return sigma * (1.0 + preact * (1.0 - sigma))


def reference(tokens, cotangent, up_first, up_second, down_first, down_second):
    block_rows = 512 if TOKENS % 512 == 0 else TOKENS
    blocks_count = TOKENS // block_rows
    first_up = up_first.astype(jnp.float32)
    second_up = up_second.astype(jnp.float32)
    first_down = down_first.astype(jnp.float32)
    second_down = down_second.astype(jnp.float32)

    def advance(totals, pair):
        token_block, grad_block = pair
        inputs = token_block.astype(jnp.float32).reshape(block_rows, DB, BLK)
        upstream = grad_block.astype(jnp.float32).reshape(block_rows, DB, BLK)
        narrow = rounded(jnp.einsum("tab,akb->tak", inputs, first_up))
        preact = jnp.einsum("tak,kac->tkc", narrow, second_up)
        hidden = rounded(jax.nn.silu(preact))
        mixed = rounded(jnp.einsum("tkc,kac->tka", hidden, first_down))
        output = (inputs + jnp.einsum("tka,akb->tab", mixed, second_down)).astype(jnp.bfloat16)
        back_mixed = rounded(jnp.einsum("tab,akb->tka", upstream, second_down))
        grad_hidden = jnp.einsum("tka,kac->tkc", back_mixed, first_down)
        grad_pre = rounded(grad_hidden * silu_slope(preact))
        back_narrow = rounded(jnp.einsum("tkc,kac->tak", grad_pre, second_up))
        grad_input = (upstream + jnp.einsum("tak,akb->tab", back_narrow, first_up)).astype(jnp.bfloat16)
        terms = (jnp.einsum("tak,tab->akb", back_narrow, inputs),
                 jnp.einsum("tak,tkc->kac", narrow, grad_pre),
                 jnp.einsum("tka,tkc->kac", back_mixed, hidden),
                 jnp.einsum("tka,tab->akb", mixed, upstream))
        totals = tuple(total + term for total, term in zip(totals, terms))
        return totals, (output.reshape(block_rows, D), grad_input.reshape(block_rows, D))

    start = (jnp.zeros((DB, HK, BLK), jnp.float32), jnp.zeros((HK, DB, BLK), jnp.float32),
             jnp.zeros((HK, DB, BLK), jnp.float32), jnp.zeros((DB, HK, BLK), jnp.float32))
    pairs = (tokens.reshape(blocks_count, block_rows, D), cotangent.reshape(blocks_count, block_rows, D))
    totals, (outputs, grad_inputs) = lax.scan(advance, start, pairs)
    factor = float(TOKENS) ** -0.5
    return (outputs.reshape(TOKENS, D), grad_inputs.reshape(TOKENS, D),
            totals[0] * factor, totals[1] * factor, totals[2] * factor, totals[3] * factor)
```

```python
import functools

import jax
import jax.numpy as jnp
from jax import lax
from jax.experimental import pallas as pl
from jax.experimental.pallas import tpu as pltpu
from jax.sharding import PartitionSpec as P

MESH = pl.DeviceIdType.MESH
F32 = jnp.float32
BF16 = jnp.bfloat16
LANES = 128
ROWS = 16


def dot(left, right, left_dim, right_dim):
    return lax.dot_general(
        left, right, (((left_dim,), (right_dim,)), ((), ())), preferred_element_type=F32
    )


def kernel(
    sizes, factor,
    x_hbm, g_hbm, u1_hbm, u2_hbm, d1_hbm, d2_hbm,
    out_hbm, gt_hbm, gu1_hbm, gu2_hbm, gd1_hbm, gd2_hbm,
    x, g, u1, u2, d1, d2, out, gt, gsum,
    send, recv, wide, nk, bk, hid, slope, gpre,
    part, packed, landed,
    in_sem, out_sem, send_sem, recv_sem, psend_sem, precv_sem,
):
    nt, nd, chunks, kd = sizes
    me = lax.axis_index("tensor")
    my_dp = lax.axis_index("dp")
    hidden_blocks = nt * kd
    tok = chunks * LANES

    barrier = pltpu.get_barrier_semaphore()

    def greet_tensor(j, carry):
        peer = lax.rem(me + j, nt)
        pl.semaphore_signal(barrier, inc=1, device_id={"tensor": peer}, device_id_type=MESH)
        return carry

    def greet_dp(j, carry):
        peer = lax.rem(my_dp + j, nd)
        pl.semaphore_signal(barrier, inc=1, device_id={"dp": peer}, device_id_type=MESH)
        return carry

    lax.fori_loop(1, nt, greet_tensor, 0)
    lax.fori_loop(1, nd, greet_dp, 0)

    loads = [
        pltpu.make_async_copy(src, dst, in_sem.at[i])
        for i, (src, dst) in enumerate(
            ((x_hbm, x), (u1_hbm, u1), (g_hbm, g), (d2_hbm, d2), (u2_hbm, u2), (d1_hbm, d1))
        )
    ]
    for load in loads:
        load.start()

    def exchange(which):
        pltpu.make_async_copy(
            send.at[which, me], recv.at[which, me], recv_sem.at[which]
        ).start()

        def one(j, carry):
            peer = lax.rem(me + j, nt)
            pltpu.make_async_remote_copy(
                src_ref=send.at[which, peer],
                dst_ref=recv.at[which, me],
                send_sem=send_sem.at[which],
                recv_sem=recv_sem.at[which],
                device_id={"tensor": peer},
                device_id_type=MESH,
            ).start()
            return carry

        lax.fori_loop(1, nt, one, 0)

    def arrived(which):
        pltpu.make_async_copy(recv.at[which], recv.at[which], recv_sem.at[which]).wait()

    def narrow_to_send(which, weight, rows):
        for tc in range(chunks):
            wide[which % 2, pl.ds(tc, hidden_blocks, stride=chunks), :] = dot(
                weight[0], rows[tc * LANES:(tc + 1) * LANES, :], 1, 1
            )
        send[which] = wide[which % 2].astype(BF16).reshape(nt, ROWS, LANES)

    def share(which):
        packed[which] = part[which].astype(BF16)

        def one(j, carry):
            peer = lax.rem(my_dp + j, nd)
            pltpu.make_async_remote_copy(
                src_ref=packed.at[which, peer],
                dst_ref=landed.at[which, my_dp],
                send_sem=psend_sem.at[which],
                recv_sem=precv_sem.at[which],
                device_id={"dp": peer},
                device_id_type=MESH,
            ).start()
            return carry

        lax.fori_loop(1, nd, one, 0)

    def reduce(which):
        others = landed.at[which, pl.ds(0, nd - 1)]
        pltpu.make_async_copy(others, others, precv_sem.at[which]).wait()
        total = part[which, my_dp]
        for j in range(1, nd):
            total = total + landed[which, lax.rem(my_dp + j, nd)].astype(F32)
        gsum[which] = total * factor

    loads[0].wait()
    loads[1].wait()
    narrow_to_send(0, u1, x)
    pl.semaphore_wait(barrier, nt + nd - 2)
    exchange(0)
    loads[2].wait()
    loads[3].wait()
    narrow_to_send(1, d2, g)
    exchange(1)
    loads[4].wait()
    loads[5].wait()

    arrived(0)
    wide[0] = recv[0].reshape(nt * ROWS, LANES).astype(F32)
    for k in range(kd):
        for tc in range(chunks):
            nk[k, :, tc * LANES:(tc + 1) * LANES] = wide[
                0, pl.ds(k * chunks + tc, nt, stride=ROWS), :
            ].astype(BF16)
        preact = dot(u2[k], nk[k], 0, 0)
        sigma = 1.0 / (1.0 + jnp.exp(-preact))
        hidden = (preact * sigma).astype(BF16)
        hid[k] = hidden
        slope[k] = sigma * (1.0 + preact * (1.0 - sigma))
        mixed = dot(d1[k], hidden, 1, 0)
        for tc in range(chunks):
            wide[1, pl.ds(k * chunks + tc, nt, stride=ROWS), :] = mixed[
                :, tc * LANES:(tc + 1) * LANES
            ]
    send[2] = wide[1].astype(BF16).reshape(nt, ROWS, LANES)
    exchange(2)

    arrived(1)
    wide[0] = recv[1].reshape(nt * ROWS, LANES).astype(F32)
    for k in range(kd):
        for tc in range(chunks):
            bk[k, :, tc * LANES:(tc + 1) * LANES] = wide[
                0, pl.ds(k * chunks + tc, nt, stride=ROWS), :
            ].astype(BF16)
        grad_pre = (dot(d1[k], bk[k], 0, 0) * slope[k]).astype(BF16)
        gpre[k] = grad_pre
        back = dot(u2[k], grad_pre, 1, 0)
        for tc in range(chunks):
            wide[1, pl.ds(k * chunks + tc, nt, stride=ROWS), :] = back[
                :, tc * LANES:(tc + 1) * LANES
            ]
    send[3] = wide[1].astype(BF16).reshape(nt, ROWS, LANES)
    exchange(3)

    share_rows = nt // nd
    for k in range(kd):
        part[1, :, k * share_rows:(k + 1) * share_rows, :] = dot(bk[k], hid[k], 1, 1).reshape(
            nd, share_rows, LANES
        )
    share(1)
    for k in range(kd):
        part[0, :, k * share_rows:(k + 1) * share_rows, :] = dot(nk[k], gpre[k], 1, 1).reshape(
            nd, share_rows, LANES
        )
    share(0)

    def back_home(which, weight, residual, other, result, slot):
        wide[which % 2] = recv[which].reshape(nt * ROWS, LANES).astype(F32)
        grad = jnp.zeros((hidden_blocks, LANES), F32)
        for tc in range(chunks):
            span = slice(tc * LANES, (tc + 1) * LANES)
            block = wide[which % 2, pl.ds(tc, hidden_blocks, stride=chunks), :].astype(BF16)
            result[span, :] = (
                residual[span, :].astype(F32) + dot(block, weight[0], 0, 0)
            ).astype(BF16)
            grad = grad + dot(block, other[span, :], 1, 0)
        part[slot] = grad.reshape(nd, hidden_blocks // nd, LANES)

    arrived(2)
    back_home(2, d2, x, g, out, 2)
    share(2)
    stores = [pltpu.make_async_copy(out, out_hbm, out_sem.at[0])]
    stores[0].start()
    reduce(1)
    reduce(0)
    for k in range(kd):
        for which, target in ((0, gu2_hbm), (1, gd1_hbm)):
            store = pltpu.make_async_copy(
                gsum.at[which, pl.ds(k * share_rows, share_rows)],
                target.at[k],
                out_sem.at[4 + which * kd + k],
            )
            store.start()
            stores.append(store)

    arrived(3)
    back_home(3, u1, g, x, gt, 3)
    share(3)
    stores.append(pltpu.make_async_copy(gt, gt_hbm, out_sem.at[1]))
    stores[-1].start()
    reduce(2)
    stores.append(pltpu.make_async_copy(gsum.at[2], gd2_hbm.at[0], out_sem.at[2]))
    stores[-1].start()
    reduce(3)
    stores.append(pltpu.make_async_copy(gsum.at[3], gu1_hbm.at[0], out_sem.at[3]))
    stores[-1].start()

    for which in range(4):
        sent = send.at[which, pl.ds(0, nt - 1)]
        pltpu.make_async_copy(sent, sent, send_sem.at[which]).wait()
        sent = packed.at[which, pl.ds(0, nd - 1)]
        pltpu.make_async_copy(sent, sent, psend_sem.at[which]).wait()
    for store in stores:
        store.wait()


def local(tokens, cotangent, up_first, up_second, down_first, down_second):
    nt, nd = lax.axis_size("tensor"), lax.axis_size("dp")
    tok, width = tokens.shape
    kd, blocks, _ = up_second.shape
    hidden_blocks = up_first.shape[1]
    chunks = tok // LANES
    slab = hidden_blocks // nd
    factor = float(tok * nd) ** -0.5
    shapes = (
        jax.ShapeDtypeStruct(tokens.shape, BF16),
        jax.ShapeDtypeStruct(tokens.shape, BF16),
        jax.ShapeDtypeStruct((1, slab, width), F32),
        jax.ShapeDtypeStruct((kd, blocks // nd, LANES), F32),
        jax.ShapeDtypeStruct((kd, blocks // nd, LANES), F32),
        jax.ShapeDtypeStruct((1, slab, width), F32),
    )
    anywhere = pl.BlockSpec(memory_space=pl.ANY)
    return pl.pallas_call(
        functools.partial(kernel, (nt, nd, chunks, kd), factor),
        out_shape=shapes,
        in_specs=[anywhere] * 6,
        out_specs=[anywhere] * 6,
        scratch_shapes=[
            pltpu.VMEM(tokens.shape, BF16),
            pltpu.VMEM(tokens.shape, BF16),
            pltpu.VMEM(up_first.shape, BF16),
            pltpu.VMEM(up_second.shape, BF16),
            pltpu.VMEM(down_first.shape, BF16),
            pltpu.VMEM(down_second.shape, BF16),
            pltpu.VMEM(tokens.shape, BF16),
            pltpu.VMEM(tokens.shape, BF16),
            pltpu.VMEM((4, slab, LANES), F32),
            pltpu.VMEM((4, nt, ROWS, LANES), BF16),
            pltpu.VMEM((4, nt, ROWS, LANES), BF16),
            pltpu.VMEM((2, nt * ROWS, LANES), F32),
            pltpu.VMEM((kd, blocks, tok), BF16),
            pltpu.VMEM((kd, blocks, tok), BF16),
            pltpu.VMEM((kd, LANES, tok), BF16),
            pltpu.VMEM((kd, LANES, tok), F32),
            pltpu.VMEM((kd, LANES, tok), BF16),
            pltpu.VMEM((4, nd, slab, LANES), F32),
            pltpu.VMEM((4, nd, slab, LANES), BF16),
            pltpu.VMEM((4, nd, slab, LANES), BF16),
            pltpu.SemaphoreType.DMA((6,)),
            pltpu.SemaphoreType.DMA((4 + 2 * kd,)),
            pltpu.SemaphoreType.DMA((4,)),
            pltpu.SemaphoreType.DMA((4,)),
            pltpu.SemaphoreType.DMA((4,)),
            pltpu.SemaphoreType.DMA((4,)),
        ],
        compiler_params=pltpu.CompilerParams(
            collective_id=0, has_side_effects=True, vmem_limit_bytes=32 * 1024 * 1024
        ),
        name="monarch",
    )(tokens, cotangent, up_first, up_second, down_first, down_second)


def solution(mesh):
    placed = (
        P("dp", "tensor"),
        P("dp", "tensor"),
        P("tensor", None, None),
        P("tensor", None, None),
        P("tensor", None, None),
        P("tensor", None, None),
    )
    return jax.shard_map(
        local,
        mesh=mesh,
        in_specs=placed,
        out_specs=(
            P("dp", "tensor"),
            P("dp", "tensor"),
            P("tensor", "dp", None),
            P("tensor", "dp", None),
            P("tensor", "dp", None),
            P("tensor", "dp", None),
        ),
        check_vma=False,
    )
```

```python
import functools

import jax
import jax.numpy as jnp
from jax import lax
from jax.experimental import pallas as pl
from jax.experimental.pallas import tpu as pltpu
from jax.sharding import PartitionSpec as P

MESH = pl.DeviceIdType.MESH
F32 = jnp.float32
BF16 = jnp.bfloat16
LANES = 128
ROWS = 16


def dot(left, right, left_dim, right_dim):
    return lax.dot_general(
        left, right, (((left_dim,), (right_dim,)), ((), ())), preferred_element_type=F32
    )


def kernel(
    sizes, factor,
    x_hbm, g_hbm, u1_hbm, u2_hbm, d1_hbm, d2_hbm,
    out, gt, gu1, gu2, gd1, gd2,
    x, g, u1, u2, d1, d2,
    send, recv, wide, nk, bk, hid, slope, gpre,
    part, packed, landed, half, half_packed, half_landed,
    in_sem, send_sem, recv_sem, psend_sem, precv_sem, hsend_sem, hrecv_sem,
):
    nt, nd, chunks, kd = sizes
    nx = nd // 2
    me = lax.axis_index("tensor")
    my_dp = lax.axis_index("dp")
    my_half = my_dp // nx
    my_x = lax.rem(my_dp, nx)
    other_half = 1 - my_half
    partner = other_half * nx + my_x
    hidden_blocks = nt * kd
    tok = chunks * LANES

    barrier = pltpu.get_barrier_semaphore()

    def greet_tensor(j, carry):
        peer = lax.rem(me + j, nt)
        pl.semaphore_signal(barrier, inc=1, device_id={"tensor": peer}, device_id_type=MESH)
        return carry

    def x_peer(j):
        return lax.rem(my_x + j, nx)

    pl.semaphore_signal(barrier, inc=1, device_id={"dp": partner}, device_id_type=MESH)
    lax.fori_loop(1, nt, greet_tensor, 0)
    for j in range(1, nx):
        pl.semaphore_signal(
            barrier, inc=1, device_id={"dp": my_half * nx + x_peer(j)}, device_id_type=MESH
        )

    loads = [
        pltpu.make_async_copy(src, dst, in_sem.at[i])
        for i, (src, dst) in enumerate(
            ((x_hbm, x), (u1_hbm, u1), (g_hbm, g), (d2_hbm, d2), (u2_hbm, u2), (d1_hbm, d1))
        )
    ]
    for load in loads:
        load.start()

    def exchange(which):
        pltpu.make_async_copy(
            send.at[which, me], recv.at[which, me], recv_sem.at[which]
        ).start()

        def one(j, carry):
            peer = lax.rem(me + j, nt)
            pltpu.make_async_remote_copy(
                src_ref=send.at[which, peer],
                dst_ref=recv.at[which, me],
                send_sem=send_sem.at[which],
                recv_sem=recv_sem.at[which],
                device_id={"tensor": peer},
                device_id_type=MESH,
            ).start()
            return carry

        lax.fori_loop(1, nt, one, 0)

    def arrived(which):
        pltpu.make_async_copy(recv.at[which], recv.at[which], recv_sem.at[which]).wait()

    def narrow_to_send(which, weight, rows):
        for tc in range(chunks):
            wide[which % 2, pl.ds(tc, hidden_blocks, stride=chunks), :] = dot(
                weight[0], rows[tc * LANES:(tc + 1) * LANES, :], 1, 1
            )
        send[which] = wide[which % 2].astype(BF16).reshape(nt, ROWS, LANES)

    def share(which):
        packed[which] = part[which].astype(BF16)
        for j in range(1, nx):
            pltpu.make_async_remote_copy(
                src_ref=packed.at[which, :, x_peer(j)],
                dst_ref=landed.at[which, my_x],
                send_sem=psend_sem.at[which],
                recv_sem=precv_sem.at[which],
                device_id={"dp": my_half * nx + x_peer(j)},
                device_id_type=MESH,
            ).start()

    def hand_over(which):
        others = landed.at[which, pl.ds(0, nx - 1)]
        pltpu.make_async_copy(others, others, precv_sem.at[which]).wait()

        def total(side):
            value = part[which, side, my_x]
            for j in range(1, nx):
                value = value + landed[which, x_peer(j), side].astype(F32)
            return value

        half_packed[which] = total(other_half).astype(BF16)
        across(which).start()
        half[which] = total(my_half)

    def across(which):
        return pltpu.make_async_remote_copy(
            src_ref=half_packed.at[which],
            dst_ref=half_landed.at[which],
            send_sem=hsend_sem.at[which],
            recv_sem=hrecv_sem.at[which],
            device_id={"dp": partner},
            device_id_type=MESH,
        )

    def finish(which, target):
        across(which).wait_recv()
        value = (half[which] + half_landed[which].astype(F32)) * factor
        target[...] = value.reshape(target.shape)

    loads[0].wait()
    loads[1].wait()
    narrow_to_send(0, u1, x)
    pl.semaphore_wait(barrier, nt - 1 + nx)
    exchange(0)
    loads[2].wait()
    loads[3].wait()
    narrow_to_send(1, d2, g)
    exchange(1)
    loads[4].wait()
    loads[5].wait()

    arrived(0)
    wide[0] = recv[0].reshape(nt * ROWS, LANES).astype(F32)
    for k in range(kd):
        for tc in range(chunks):
            nk[k, :, tc * LANES:(tc + 1) * LANES] = wide[
                0, pl.ds(k * chunks + tc, nt, stride=ROWS), :
            ].astype(BF16)
        preact = dot(u2[k], nk[k], 0, 0)
        sigma = 1.0 / (1.0 + jnp.exp(-preact))
        hidden = (preact * sigma).astype(BF16)
        hid[k] = hidden
        slope[k] = sigma * (1.0 + preact * (1.0 - sigma))
        mixed = dot(d1[k], hidden, 1, 0)
        for tc in range(chunks):
            wide[1, pl.ds(k * chunks + tc, nt, stride=ROWS), :] = mixed[
                :, tc * LANES:(tc + 1) * LANES
            ]
    send[2] = wide[1].astype(BF16).reshape(nt, ROWS, LANES)
    exchange(2)

    arrived(1)
    wide[0] = recv[1].reshape(nt * ROWS, LANES).astype(F32)
    for k in range(kd):
        for tc in range(chunks):
            bk[k, :, tc * LANES:(tc + 1) * LANES] = wide[
                0, pl.ds(k * chunks + tc, nt, stride=ROWS), :
            ].astype(BF16)
        grad_pre = (dot(d1[k], bk[k], 0, 0) * slope[k]).astype(BF16)
        gpre[k] = grad_pre
        back = dot(u2[k], grad_pre, 1, 0)
        for tc in range(chunks):
            wide[1, pl.ds(k * chunks + tc, nt, stride=ROWS), :] = back[
                :, tc * LANES:(tc + 1) * LANES
            ]
    send[3] = wide[1].astype(BF16).reshape(nt, ROWS, LANES)
    exchange(3)

    share_rows = nt // nd
    for k in range(kd):
        part[1, :, :, k * share_rows:(k + 1) * share_rows, :] = dot(bk[k], hid[k], 1, 1).reshape(
            2, nx, share_rows, LANES
        )
    share(1)
    for k in range(kd):
        part[0, :, :, k * share_rows:(k + 1) * share_rows, :] = dot(nk[k], gpre[k], 1, 1).reshape(
            2, nx, share_rows, LANES
        )
    share(0)

    def back_home(which, weight, residual, other, result, slot):
        wide[which % 2] = recv[which].reshape(nt * ROWS, LANES).astype(F32)
        grad = jnp.zeros((hidden_blocks, LANES), F32)
        for tc in range(chunks):
            span = slice(tc * LANES, (tc + 1) * LANES)
            block = wide[which % 2, pl.ds(tc, hidden_blocks, stride=chunks), :].astype(BF16)
            result[span, :] = (
                residual[span, :].astype(F32) + dot(block, weight[0], 0, 0)
            ).astype(BF16)
            grad = grad + dot(block, other[span, :], 1, 0)
        part[slot] = grad.reshape(2, nx, hidden_blocks // nd, LANES)

    arrived(2)
    back_home(2, d2, x, g, out, 2)
    share(2)
    hand_over(1)
    hand_over(0)
    hand_over(2)
    finish(1, gd1)
    finish(0, gu2)

    arrived(3)
    back_home(3, u1, g, x, gt, 3)
    share(3)
    finish(2, gd2)
    hand_over(3)
    finish(3, gu1)

    for which in range(4):
        sent = send.at[which, pl.ds(0, nt - 1)]
        pltpu.make_async_copy(sent, sent, send_sem.at[which]).wait()
        sent = packed.at[which, :, pl.ds(0, nx - 1)]
        pltpu.make_async_copy(sent, sent, psend_sem.at[which]).wait()
        across(which).wait_send()


def write_out(*refs):
    count = len(refs) // 2
    sems = refs[-1]
    copies = [
        pltpu.make_async_copy(refs[i], refs[count + i], sems.at[i]) for i in range(count)
    ]
    for copy in copies:
        copy.start()
    for copy in copies:
        copy.wait()


def local(tokens, cotangent, up_first, up_second, down_first, down_second):
    nt, nd = lax.axis_size("tensor"), lax.axis_size("dp")
    tok, width = tokens.shape
    kd, blocks, _ = up_second.shape
    hidden_blocks = up_first.shape[1]
    chunks = tok // LANES
    slab = hidden_blocks // nd
    factor = float(tok * nd) ** -0.5
    shapes = (
        jax.ShapeDtypeStruct(tokens.shape, BF16),
        jax.ShapeDtypeStruct(tokens.shape, BF16),
        jax.ShapeDtypeStruct((1, slab, width), F32),
        jax.ShapeDtypeStruct((kd, blocks // nd, LANES), F32),
        jax.ShapeDtypeStruct((kd, blocks // nd, LANES), F32),
        jax.ShapeDtypeStruct((1, slab, width), F32),
    )
    in_hbm = pl.BlockSpec(memory_space=pltpu.HBM)
    in_vmem = pl.BlockSpec(memory_space=pltpu.VMEM)
    results = pl.pallas_call(
        functools.partial(kernel, (nt, nd, chunks, kd), factor),
        out_shape=shapes,
        in_specs=[in_hbm] * 6,
        out_specs=[in_vmem] * 6,
        scratch_shapes=[
            pltpu.VMEM(tokens.shape, BF16),
            pltpu.VMEM(tokens.shape, BF16),
            pltpu.VMEM(up_first.shape, BF16),
            pltpu.VMEM(up_second.shape, BF16),
            pltpu.VMEM(down_first.shape, BF16),
            pltpu.VMEM(down_second.shape, BF16),
            pltpu.VMEM((4, nt, ROWS, LANES), BF16),
            pltpu.VMEM((4, nt, ROWS, LANES), BF16),
            pltpu.VMEM((2, nt * ROWS, LANES), F32),
            pltpu.VMEM((kd, blocks, tok), BF16),
            pltpu.VMEM((kd, blocks, tok), BF16),
            pltpu.VMEM((kd, LANES, tok), BF16),
            pltpu.VMEM((kd, LANES, tok), F32),
            pltpu.VMEM((kd, LANES, tok), BF16),
            pltpu.VMEM((4, 2, nd // 2, slab, LANES), F32),
            pltpu.VMEM((4, 2, nd // 2, slab, LANES), BF16),
            pltpu.VMEM((4, nd // 2, 2, slab, LANES), BF16),
            pltpu.VMEM((4, slab, LANES), F32),
            pltpu.VMEM((4, slab, LANES), BF16),
            pltpu.VMEM((4, slab, LANES), BF16),
            pltpu.SemaphoreType.DMA((6,)),
            pltpu.SemaphoreType.DMA((4,)),
            pltpu.SemaphoreType.DMA((4,)),
            pltpu.SemaphoreType.DMA((4,)),
            pltpu.SemaphoreType.DMA((4,)),
            pltpu.SemaphoreType.DMA((4,)),
            pltpu.SemaphoreType.DMA((4,)),
        ],
        compiler_params=pltpu.CompilerParams(
            collective_id=0, has_side_effects=True, vmem_limit_bytes=63 * 1024 * 1024
        ),
        name="monarch",
    )(tokens, cotangent, up_first, up_second, down_first, down_second)
    return pl.pallas_call(
        write_out,
        out_shape=shapes,
        in_specs=[in_vmem] * 6,
        out_specs=[in_hbm] * 6,
        scratch_shapes=[pltpu.SemaphoreType.DMA((6,))],
        name="write_out",
    )(*results)


def solution(mesh):
    placed = (
        P("dp", "tensor"),
        P("dp", "tensor"),
        P("tensor", None, None),
        P("tensor", None, None),
        P("tensor", None, None),
        P("tensor", None, None),
    )
    return jax.shard_map(
        local,
        mesh=mesh,
        in_specs=placed,
        out_specs=(
            P("dp", "tensor"),
            P("dp", "tensor"),
            P("tensor", "dp", None),
            P("tensor", "dp", None),
            P("tensor", "dp", None),
            P("tensor", "dp", None),
        ),
        check_vma=False,
    )
```

```python
import functools

import jax
import jax.numpy as jnp
from jax import lax
from jax.experimental import pallas as pl
from jax.experimental.pallas import tpu as pltpu
from jax.sharding import PartitionSpec as P

MESH = pl.DeviceIdType.MESH
F32 = jnp.float32
BF16 = jnp.bfloat16
LANES = 128
ROWS = 16


def dot(left, right, left_dim, right_dim):
    return lax.dot_general(
        left, right, (((left_dim,), (right_dim,)), ((), ())), preferred_element_type=F32
    )


def kernel(
    sizes, factor,
    x_hbm, g_hbm, u1_hbm, u2_hbm, d1_hbm, d2_hbm,
    out, gt, gu1, gu2, gd1, gd2,
    x, g, u1, u2, d1, d2,
    send, recv, wide, nk, bk, hid, slope, gpre,
    home, part, packed, landed, half, half_packed, half_landed,
    in_sem, send_sem, recv_sem, psend_sem, precv_sem, hsend_sem, hrecv_sem,
):
    nt, nd, chunks, kd = sizes
    nx = nd // 2
    me = lax.axis_index("tensor")
    my_dp = lax.axis_index("dp")
    my_half = my_dp // nx
    my_x = lax.rem(my_dp, nx)
    other_half = 1 - my_half
    partner = other_half * nx + my_x
    hidden_blocks = nt * kd
    tok = chunks * LANES

    barrier = pltpu.get_barrier_semaphore()
    step = jnp.where(me >= nt // 2, 1, -1)

    def tensor_peer(j):
        return lax.rem(me + nt + step * j, nt)

    def greet_tensor(j, carry):
        peer = tensor_peer(j)
        pl.semaphore_signal(barrier, inc=1, device_id={"tensor": peer}, device_id_type=MESH)
        return carry

    def x_peer(j):
        return lax.rem(my_x + j, nx)

    pl.semaphore_signal(barrier, inc=1, device_id={"dp": partner}, device_id_type=MESH)
    lax.fori_loop(1, nt, greet_tensor, 0)
    for j in range(1, nx):
        pl.semaphore_signal(
            barrier, inc=1, device_id={"dp": my_half * nx + x_peer(j)}, device_id_type=MESH
        )

    loads = [
        pltpu.make_async_copy(src, dst, in_sem.at[i])
        for i, (src, dst) in enumerate(
            ((x_hbm, x), (u1_hbm, u1), (g_hbm, g), (d2_hbm, d2), (u2_hbm, u2), (d1_hbm, d1))
        )
    ]
    for load in loads:
        load.start()

    def exchange(which):
        pltpu.make_async_copy(
            send.at[which, me], recv.at[which, me], recv_sem.at[which]
        ).start()

        def one(j, carry):
            peer = tensor_peer(j)
            pltpu.make_async_remote_copy(
                src_ref=send.at[which, peer],
                dst_ref=recv.at[which, me],
                send_sem=send_sem.at[which],
                recv_sem=recv_sem.at[which],
                device_id={"tensor": peer},
                device_id_type=MESH,
            ).start()
            return carry

        lax.fori_loop(1, nt, one, 0)

    def arrived(which):
        pltpu.make_async_copy(recv.at[which], recv.at[which], recv_sem.at[which]).wait()

    def narrow_to_send(which, weight, rows):
        for tc in range(chunks):
            wide[which % 2, pl.ds(tc, hidden_blocks, stride=chunks), :] = dot(
                weight[0], rows[tc * LANES:(tc + 1) * LANES, :], 1, 1
            )
        send[which] = wide[which % 2].astype(BF16).reshape(nt, ROWS, LANES)

    def share(which):
        packed[which] = part[which].astype(BF16)
        for j in range(1, nx):
            pltpu.make_async_remote_copy(
                src_ref=packed.at[which, :, x_peer(j)],
                dst_ref=landed.at[which, my_x],
                send_sem=psend_sem.at[which],
                recv_sem=precv_sem.at[which],
                device_id={"dp": my_half * nx + x_peer(j)},
                device_id_type=MESH,
            ).start()

    def hand_over(which):
        others = landed.at[which, pl.ds(0, nx - 1)]
        pltpu.make_async_copy(others, others, precv_sem.at[which]).wait()

        def total(side):
            value = part[which, side, my_x]
            for j in range(1, nx):
                value = value + landed[which, x_peer(j), side].astype(F32)
            return value

        half_packed[which] = total(other_half).astype(BF16)
        across(which).start()
        half[which] = total(my_half)

    def across(which):
        return pltpu.make_async_remote_copy(
            src_ref=half_packed.at[which],
            dst_ref=half_landed.at[which],
            send_sem=hsend_sem.at[which],
            recv_sem=hrecv_sem.at[which],
            device_id={"dp": partner},
            device_id_type=MESH,
        )

    def finish(which, target):
        across(which).wait_recv()
        value = (half[which] + half_landed[which].astype(F32)) * factor
        target[...] = value.reshape(target.shape)

    loads[0].wait()
    loads[1].wait()
    narrow_to_send(0, u1, x)
    pl.semaphore_wait(barrier, nt - 1 + nx)
    exchange(0)
    loads[2].wait()
    loads[3].wait()
    narrow_to_send(1, d2, g)
    exchange(1)
    loads[4].wait()
    loads[5].wait()

    arrived(0)
    wide[0] = recv[0].reshape(nt * ROWS, LANES).astype(F32)
    for k in range(kd):
        for tc in range(chunks):
            nk[k, :, tc * LANES:(tc + 1) * LANES] = wide[
                0, pl.ds(k * chunks + tc, nt, stride=ROWS), :
            ].astype(BF16)
        preact = dot(u2[k], nk[k], 0, 0)
        sigma = 1.0 / (1.0 + jnp.exp(-preact))
        hidden = (preact * sigma).astype(BF16)
        hid[k] = hidden
        slope[k] = sigma * (1.0 + preact * (1.0 - sigma))
        mixed = dot(d1[k], hidden, 1, 0)
        for tc in range(chunks):
            wide[1, pl.ds(k * chunks + tc, nt, stride=ROWS), :] = mixed[
                :, tc * LANES:(tc + 1) * LANES
            ]
    send[2] = wide[1].astype(BF16).reshape(nt, ROWS, LANES)
    exchange(2)

    arrived(1)
    wide[0] = recv[1].reshape(nt * ROWS, LANES).astype(F32)
    for k in range(kd):
        for tc in range(chunks):
            bk[k, :, tc * LANES:(tc + 1) * LANES] = wide[
                0, pl.ds(k * chunks + tc, nt, stride=ROWS), :
            ].astype(BF16)
        grad_pre = (dot(d1[k], bk[k], 0, 0) * slope[k]).astype(BF16)
        gpre[k] = grad_pre
        back = dot(u2[k], grad_pre, 1, 0)
        for tc in range(chunks):
            wide[1, pl.ds(k * chunks + tc, nt, stride=ROWS), :] = back[
                :, tc * LANES:(tc + 1) * LANES
            ]
    send[3] = wide[1].astype(BF16).reshape(nt, ROWS, LANES)
    exchange(3)

    share_rows = nt // nd
    for k in range(kd):
        part[1, :, :, k * share_rows:(k + 1) * share_rows, :] = dot(bk[k], hid[k], 1, 1).reshape(
            2, nx, share_rows, LANES
        )
    share(1)
    for k in range(kd):
        part[0, :, :, k * share_rows:(k + 1) * share_rows, :] = dot(nk[k], gpre[k], 1, 1).reshape(
            2, nx, share_rows, LANES
        )
    share(0)

    def unpack(which):
        wide[which % 2] = recv[which].reshape(nt * ROWS, LANES).astype(F32)
        for tc in range(chunks):
            home[which % 2, tc] = wide[
                which % 2, pl.ds(tc, hidden_blocks, stride=chunks), :
            ].astype(BF16)

    def factor_grad(which, other):
        grad = jnp.zeros((hidden_blocks, LANES), F32)
        for tc in range(chunks):
            grad = grad + dot(home[which % 2, tc], other[tc * LANES:(tc + 1) * LANES, :], 1, 0)
        part[which] = grad.reshape(2, nx, hidden_blocks // nd, LANES)

    def leave(which, weight, residual, result):
        for tc in range(chunks):
            span = slice(tc * LANES, (tc + 1) * LANES)
            result[span, :] = (
                residual[span, :].astype(F32) + dot(home[which % 2, tc], weight[0], 0, 0)
            ).astype(BF16)

    arrived(2)
    unpack(2)
    factor_grad(2, g)
    share(2)
    leave(2, d2, x, out)

    arrived(3)
    unpack(3)
    factor_grad(3, x)
    share(3)
    hand_over(1)
    hand_over(0)
    hand_over(2)
    leave(3, u1, g, gt)
    hand_over(3)
    finish(1, gd1)
    finish(0, gu2)
    finish(2, gd2)
    finish(3, gu1)

    for which in range(4):
        sent = send.at[which, pl.ds(0, nt - 1)]
        pltpu.make_async_copy(sent, sent, send_sem.at[which]).wait()
        sent = packed.at[which, :, pl.ds(0, nx - 1)]
        pltpu.make_async_copy(sent, sent, psend_sem.at[which]).wait()
        across(which).wait_send()


def write_out(*refs):
    count = len(refs) // 2
    sems = refs[-1]
    copies = [
        pltpu.make_async_copy(refs[i], refs[count + i], sems.at[i]) for i in range(count)
    ]
    for copy in copies:
        copy.start()
    for copy in copies:
        copy.wait()


def local(tokens, cotangent, up_first, up_second, down_first, down_second):
    nt, nd = lax.axis_size("tensor"), lax.axis_size("dp")
    tok, width = tokens.shape
    kd, blocks, _ = up_second.shape
    hidden_blocks = up_first.shape[1]
    chunks = tok // LANES
    slab = hidden_blocks // nd
    factor = float(tok * nd) ** -0.5
    shapes = (
        jax.ShapeDtypeStruct(tokens.shape, BF16),
        jax.ShapeDtypeStruct(tokens.shape, BF16),
        jax.ShapeDtypeStruct((1, slab, width), F32),
        jax.ShapeDtypeStruct((kd, blocks // nd, LANES), F32),
        jax.ShapeDtypeStruct((kd, blocks // nd, LANES), F32),
        jax.ShapeDtypeStruct((1, slab, width), F32),
    )
    in_vmem = pl.BlockSpec(memory_space=pltpu.VMEM)
    in_hbm = pl.BlockSpec(memory_space=pltpu.HBM)
    results = pl.pallas_call(
        functools.partial(kernel, (nt, nd, chunks, kd), factor),
        out_shape=shapes,
        in_specs=[in_hbm] * 6,
        out_specs=[in_vmem] * 6,
        scratch_shapes=[
            pltpu.VMEM(tokens.shape, BF16),
            pltpu.VMEM(tokens.shape, BF16),
            pltpu.VMEM(up_first.shape, BF16),
            pltpu.VMEM(up_second.shape, BF16),
            pltpu.VMEM(down_first.shape, BF16),
            pltpu.VMEM(down_second.shape, BF16),
            pltpu.VMEM((4, nt, ROWS, LANES), BF16),
            pltpu.VMEM((4, nt, ROWS, LANES), BF16),
            pltpu.VMEM((2, nt * ROWS, LANES), F32),
            pltpu.VMEM((kd, blocks, tok), BF16),
            pltpu.VMEM((kd, blocks, tok), BF16),
            pltpu.VMEM((kd, LANES, tok), BF16),
            pltpu.VMEM((kd, LANES, tok), F32),
            pltpu.VMEM((kd, LANES, tok), BF16),
            pltpu.VMEM((2, chunks, hidden_blocks, LANES), BF16),
            pltpu.VMEM((4, 2, nd // 2, slab, LANES), F32),
            pltpu.VMEM((4, 2, nd // 2, slab, LANES), BF16),
            pltpu.VMEM((4, nd // 2, 2, slab, LANES), BF16),
            pltpu.VMEM((4, slab, LANES), F32),
            pltpu.VMEM((4, slab, LANES), BF16),
            pltpu.VMEM((4, slab, LANES), BF16),
            pltpu.SemaphoreType.DMA((6,)),
            pltpu.SemaphoreType.DMA((4,)),
            pltpu.SemaphoreType.DMA((4,)),
            pltpu.SemaphoreType.DMA((4,)),
            pltpu.SemaphoreType.DMA((4,)),
            pltpu.SemaphoreType.DMA((4,)),
            pltpu.SemaphoreType.DMA((4,)),
        ],
        compiler_params=pltpu.CompilerParams(
            collective_id=0, has_side_effects=True, vmem_limit_bytes=63 * 1024 * 1024
        ),
        name="monarch",
    )(tokens, cotangent, up_first, up_second, down_first, down_second)
    return pl.pallas_call(
        write_out,
        out_shape=shapes,
        in_specs=[in_vmem] * 6,
        out_specs=[in_hbm] * 6,
        scratch_shapes=[pltpu.SemaphoreType.DMA((6,))],
        name="write_out",
    )(*results)


def solution(mesh):
    placed = (
        P("dp", "tensor"),
        P("dp", "tensor"),
        P("tensor", None, None),
        P("tensor", None, None),
        P("tensor", None, None),
        P("tensor", None, None),
    )
    return jax.shard_map(
        local,
        mesh=mesh,
        in_specs=placed,
        out_specs=(
            P("dp", "tensor"),
            P("dp", "tensor"),
            P("tensor", "dp", None),
            P("tensor", "dp", None),
            P("tensor", "dp", None),
            P("tensor", "dp", None),
        ),
        check_vma=False,
    )
```

```python
import functools

import jax
import jax.numpy as jnp
from jax import lax
from jax.experimental import pallas as pl
from jax.experimental.pallas import tpu as pltpu
from jax.sharding import PartitionSpec as P

MESH = pl.DeviceIdType.MESH
F32 = jnp.float32
BF16 = jnp.bfloat16
LANES = 128
ROWS = 16


def dot(left, right, left_dim, right_dim):
    return lax.dot_general(
        left, right, (((left_dim,), (right_dim,)), ((), ())), preferred_element_type=F32
    )


def kernel(
    sizes, factor,
    x_hbm, g_hbm, u1_hbm, u2_hbm, d1_hbm, d2_hbm,
    out_hbm, gt_hbm, gu1_hbm, gu2_hbm, gd1_hbm, gd2_hbm,
    x, g, u1, u2, d1, d2, out, gt, gsum,
    send, recv, wide, nk, bk, hid, slope, gpre,
    home, part, packed, landed, direct, half, half_packed, half_landed,
    in_sem, out_sem, send_sem, recv_sem, psend_sem, precv_sem, hsend_sem, hrecv_sem,
):
    nt, nd, chunks, kd = sizes
    nx = nd // 2
    me = lax.axis_index("tensor")
    my_dp = lax.axis_index("dp")
    my_half = my_dp // nx
    my_x = lax.rem(my_dp, nx)
    other_half = 1 - my_half
    partner = other_half * nx + my_x
    run_half = me // (nt // 2)
    sides = (run_half, 1 - run_half)
    hidden_blocks = nt * kd
    tok = chunks * LANES

    barrier = pltpu.get_barrier_semaphore()
    step = jnp.where(me >= nt // 2, 1, -1)

    def tensor_peer(j):
        return lax.rem(me + nt + step * j, nt)

    def greet_tensor(j, carry):
        peer = tensor_peer(j)
        pl.semaphore_signal(barrier, inc=1, device_id={"tensor": peer}, device_id_type=MESH)
        return carry

    def x_peer(j):
        return lax.rem(my_x + j, nx)

    for j in range(nx):
        pl.semaphore_signal(
            barrier, inc=1, device_id={"dp": other_half * nx + x_peer(j)}, device_id_type=MESH
        )
    lax.fori_loop(1, nt, greet_tensor, 0)
    for j in range(1, nx):
        pl.semaphore_signal(
            barrier, inc=1, device_id={"dp": my_half * nx + x_peer(j)}, device_id_type=MESH
        )

    loads = [
        pltpu.make_async_copy(src, dst, in_sem.at[i])
        for i, (src, dst) in enumerate(
            ((x_hbm, x), (u1_hbm, u1), (g_hbm, g), (d2_hbm, d2), (u2_hbm, u2), (d1_hbm, d1))
        )
    ]
    for load in loads:
        load.start()

    def exchange(which):
        pltpu.make_async_copy(
            send.at[which, me], recv.at[which, me], recv_sem.at[which]
        ).start()

        def one(j, carry):
            peer = tensor_peer(j)
            side = lax.rem(peer // (nt // 2) + run_half, 2) if which == 3 else 0
            pltpu.make_async_remote_copy(
                src_ref=send.at[which, peer],
                dst_ref=recv.at[which, me],
                send_sem=send_sem.at[which],
                recv_sem=recv_sem.at[which + side],
                device_id={"tensor": peer},
                device_id_type=MESH,
            ).start()
            return carry

        lax.fori_loop(1, nt, one, 0)

    def arrived(which):
        pltpu.make_async_copy(recv.at[which], recv.at[which], recv_sem.at[which]).wait()

    def narrow_to_send(which, weight, rows):
        for tc in range(chunks):
            wide[which % 2, pl.ds(tc, hidden_blocks, stride=chunks), :] = dot(
                weight[0], rows[tc * LANES:(tc + 1) * LANES, :], 1, 1
            )
        send[which] = wide[which % 2].astype(BF16).reshape(nt, ROWS, LANES)

    def share(which):
        packed[which] = part[which].astype(BF16)
        for j in range(1, nx):
            pltpu.make_async_remote_copy(
                src_ref=packed.at[which, :, x_peer(j)],
                dst_ref=landed.at[which, my_x],
                send_sem=psend_sem.at[which],
                recv_sem=precv_sem.at[which],
                device_id={"dp": my_half * nx + x_peer(j)},
                device_id_type=MESH,
            ).start()

    def hand_over(which):
        others = landed.at[which, pl.ds(0, nx - 1)]
        pltpu.make_async_copy(others, others, precv_sem.at[which]).wait()

        def total(side):
            value = part[which, side, my_x]
            for j in range(1, nx):
                value = value + landed[which, x_peer(j), side].astype(F32)
            return value

        half_packed[which] = total(other_half).astype(BF16)
        across(which).start()
        half[which] = total(my_half)

    def across(which):
        return pltpu.make_async_remote_copy(
            src_ref=half_packed.at[which],
            dst_ref=half_landed.at[which],
            send_sem=hsend_sem.at[which],
            recv_sem=hrecv_sem.at[which],
            device_id={"dp": partner},
            device_id_type=MESH,
        )

    def finish(which):
        across(which).wait_recv()
        gsum[which] = (half[which] + half_landed[which].astype(F32)) * factor

    def finish_direct():
        others = direct.at[pl.ds(0, nd - 1)]
        pltpu.make_async_copy(others, others, precv_sem.at[3]).wait()
        value = part[3, my_half, my_x]
        for j in range(1, nd):
            value = value + direct[lax.rem(my_dp + j, nd)].astype(F32)
        gsum[3] = value * factor

    stores = []

    def store(src, dst):
        copy = pltpu.make_async_copy(src, dst, out_sem.at[len(stores)])
        copy.start()
        stores.append(copy)

    def store_sum(which, target):
        for k in range(kd):
            store(gsum.at[which, pl.ds(k * share_rows, share_rows)], target.at[k])

    loads[0].wait()
    loads[1].wait()
    narrow_to_send(0, u1, x)
    pl.semaphore_wait(barrier, nt - 1 + nd - 1)
    exchange(0)
    loads[2].wait()
    loads[3].wait()
    narrow_to_send(1, d2, g)
    exchange(1)
    loads[4].wait()
    loads[5].wait()

    arrived(0)
    wide[0] = recv[0].reshape(nt * ROWS, LANES).astype(F32)
    for k in range(kd):
        for tc in range(chunks):
            nk[k, :, tc * LANES:(tc + 1) * LANES] = wide[
                0, pl.ds(k * chunks + tc, nt, stride=ROWS), :
            ].astype(BF16)
        preact = dot(u2[k], nk[k], 0, 0)
        sigma = 1.0 / (1.0 + jnp.exp(-preact))
        hidden = (preact * sigma).astype(BF16)
        hid[k] = hidden
        slope[k] = sigma * (1.0 + preact * (1.0 - sigma))
        mixed = dot(d1[k], hidden, 1, 0)
        for tc in range(chunks):
            wide[1, pl.ds(k * chunks + tc, nt, stride=ROWS), :] = mixed[
                :, tc * LANES:(tc + 1) * LANES
            ]
    send[2] = wide[1].astype(BF16).reshape(nt, ROWS, LANES)
    exchange(2)

    arrived(1)
    wide[0] = recv[1].reshape(nt * ROWS, LANES).astype(F32)
    for k in range(kd):
        for tc in range(chunks):
            bk[k, :, tc * LANES:(tc + 1) * LANES] = wide[
                0, pl.ds(k * chunks + tc, nt, stride=ROWS), :
            ].astype(BF16)
        grad_pre = (dot(d1[k], bk[k], 0, 0) * slope[k]).astype(BF16)
        gpre[k] = grad_pre
        back = dot(u2[k], grad_pre, 1, 0)
        for tc in range(chunks):
            wide[1, pl.ds(k * chunks + tc, nt, stride=ROWS), :] = back[
                :, tc * LANES:(tc + 1) * LANES
            ]
    send[3] = wide[1].astype(BF16).reshape(nt, ROWS, LANES)
    exchange(3)

    share_rows = nt // nd
    for k in range(kd):
        part[1, :, :, k * share_rows:(k + 1) * share_rows, :] = dot(bk[k], hid[k], 1, 1).reshape(
            2, nx, share_rows, LANES
        )
    share(1)
    for k in range(kd):
        part[0, :, :, k * share_rows:(k + 1) * share_rows, :] = dot(nk[k], gpre[k], 1, 1).reshape(
            2, nx, share_rows, LANES
        )
    share(0)

    def unpack(which):
        wide[which % 2] = recv[which].reshape(nt * ROWS, LANES).astype(F32)
        for tc in range(chunks):
            home[which % 2, tc] = wide[
                which % 2, pl.ds(tc, hidden_blocks, stride=chunks), :
            ].astype(BF16)

    def factor_grad(which, other):
        grad = jnp.zeros((hidden_blocks, LANES), F32)
        for tc in range(chunks):
            grad = grad + dot(home[which % 2, tc], other[tc * LANES:(tc + 1) * LANES, :], 1, 0)
        part[which] = grad.reshape(2, nx, hidden_blocks // nd, LANES)

    def leave(which, weight, residual, result):
        for tc in range(chunks):
            span = slice(tc * LANES, (tc + 1) * LANES)
            result[span, :] = (
                residual[span, :].astype(F32) + dot(home[which % 2, tc], weight[0], 0, 0)
            ).astype(BF16)

    def arrived_side(side):
        block = recv.at[3, pl.ds(sides[side] * (nt // 2), nt // 2)]
        pltpu.make_async_copy(block, block, recv_sem.at[3 + side]).wait()

    def unpack_side(side):
        count = nt * ROWS // 2
        block = recv[3, pl.ds(sides[side] * (nt // 2), nt // 2)]
        wide[1, side * count:(side + 1) * count, :] = block.reshape(count, LANES).astype(F32)
        for tc in range(chunks):
            home[1, tc, side_rows(side), :] = wide[
                1, pl.ds(side * count + tc, hidden_blocks // 2, stride=chunks), :
            ].astype(BF16)

    def side_rows(side):
        return slice(side * hidden_blocks // 2, (side + 1) * hidden_blocks // 2)

    def share_side(side):
        target = sides[side]
        grad = jnp.zeros((hidden_blocks // 2, LANES), F32)
        for tc in range(chunks):
            span = slice(tc * LANES, (tc + 1) * LANES)
            grad = grad + dot(home[1, tc, side_rows(side), :], x[span, :], 1, 0)
        grad = grad.reshape(nx, hidden_blocks // nd, LANES)
        part[3, target] = grad
        packed[3, target] = grad.astype(BF16)
        for j in range(nx):
            copy = pltpu.make_async_remote_copy(
                src_ref=packed.at[3, target, x_peer(j)],
                dst_ref=direct.at[my_dp],
                send_sem=psend_sem.at[3],
                recv_sem=precv_sem.at[3],
                device_id={"dp": target * nx + x_peer(j)},
                device_id_type=MESH,
            )
            if j > 0:
                copy.start()
            else:
                pl.when(target != my_half)(copy.start)

    arrived(2)
    unpack(2)
    factor_grad(2, g)
    share(2)
    leave(2, d2, x, out)
    store(out, out_hbm)

    for side in range(2):
        arrived_side(side)
        unpack_side(side)
        share_side(side)
    hand_over(1)
    hand_over(0)
    hand_over(2)
    for tc in range(chunks):
        span = slice(tc * LANES, (tc + 1) * LANES)
        value = g[span, :].astype(F32)
        for side in range(2):
            rows = pl.ds(sides[side] * (hidden_blocks // 2), hidden_blocks // 2)
            value = value + dot(home[1, tc, side_rows(side), :], u1[0, rows, :], 0, 0)
        gt[span, :] = value.astype(BF16)
    store(gt, gt_hbm)
    finish(1)
    store_sum(1, gd1_hbm)
    finish(0)
    store_sum(0, gu2_hbm)
    finish(2)
    store(gsum.at[2], gd2_hbm.at[0])
    finish_direct()
    store(gsum.at[3], gu1_hbm.at[0])

    for which in range(4):
        sent = send.at[which, pl.ds(0, nt - 1)]
        pltpu.make_async_copy(sent, sent, send_sem.at[which]).wait()
    for which in range(3):
        sent = packed.at[which, :, pl.ds(0, nx - 1)]
        pltpu.make_async_copy(sent, sent, psend_sem.at[which]).wait()
        across(which).wait_send()
    sent = direct.at[pl.ds(0, nd - 1)]
    pltpu.make_async_copy(sent, sent, psend_sem.at[3]).wait()
    for copy in stores:
        copy.wait()


def write_out(*refs):
    count = len(refs) // 2
    sems = refs[-1]
    copies = [
        pltpu.make_async_copy(refs[i], refs[count + i], sems.at[i]) for i in range(count)
    ]
    for copy in copies:
        copy.start()
    for copy in copies:
        copy.wait()


def local(tokens, cotangent, up_first, up_second, down_first, down_second):
    nt, nd = lax.axis_size("tensor"), lax.axis_size("dp")
    tok, width = tokens.shape
    kd, blocks, _ = up_second.shape
    hidden_blocks = up_first.shape[1]
    chunks = tok // LANES
    slab = hidden_blocks // nd
    factor = float(tok * nd) ** -0.5
    shapes = (
        jax.ShapeDtypeStruct(tokens.shape, BF16),
        jax.ShapeDtypeStruct(tokens.shape, BF16),
        jax.ShapeDtypeStruct((1, slab, width), F32),
        jax.ShapeDtypeStruct((kd, blocks // nd, LANES), F32),
        jax.ShapeDtypeStruct((kd, blocks // nd, LANES), F32),
        jax.ShapeDtypeStruct((1, slab, width), F32),
    )
    in_vmem = pl.BlockSpec(memory_space=pltpu.VMEM)
    in_hbm = pl.BlockSpec(memory_space=pltpu.HBM)
    results = pl.pallas_call(
        functools.partial(kernel, (nt, nd, chunks, kd), factor),
        out_shape=shapes,
        in_specs=[in_hbm] * 6,
        out_specs=[in_hbm] * 6,
        scratch_shapes=[
            pltpu.VMEM(tokens.shape, BF16),
            pltpu.VMEM(tokens.shape, BF16),
            pltpu.VMEM(up_first.shape, BF16),
            pltpu.VMEM(up_second.shape, BF16),
            pltpu.VMEM(down_first.shape, BF16),
            pltpu.VMEM(down_second.shape, BF16),
            pltpu.VMEM(tokens.shape, BF16),
            pltpu.VMEM(tokens.shape, BF16),
            pltpu.VMEM((4, slab, LANES), F32),
            pltpu.VMEM((4, nt, ROWS, LANES), BF16),
            pltpu.VMEM((4, nt, ROWS, LANES), BF16),
            pltpu.VMEM((2, nt * ROWS, LANES), F32),
            pltpu.VMEM((kd, blocks, tok), BF16),
            pltpu.VMEM((kd, blocks, tok), BF16),
            pltpu.VMEM((kd, LANES, tok), BF16),
            pltpu.VMEM((kd, LANES, tok), F32),
            pltpu.VMEM((kd, LANES, tok), BF16),
            pltpu.VMEM((2, chunks, hidden_blocks, LANES), BF16),
            pltpu.VMEM((4, 2, nd // 2, slab, LANES), F32),
            pltpu.VMEM((4, 2, nd // 2, slab, LANES), BF16),
            pltpu.VMEM((3, nd // 2, 2, slab, LANES), BF16),
            pltpu.VMEM((nd, slab, LANES), BF16),
            pltpu.VMEM((3, slab, LANES), F32),
            pltpu.VMEM((3, slab, LANES), BF16),
            pltpu.VMEM((3, slab, LANES), BF16),
            pltpu.SemaphoreType.DMA((6,)),
            pltpu.SemaphoreType.DMA((4 + 2 * kd,)),
            pltpu.SemaphoreType.DMA((4,)),
            pltpu.SemaphoreType.DMA((5,)),
            pltpu.SemaphoreType.DMA((4,)),
            pltpu.SemaphoreType.DMA((4,)),
            pltpu.SemaphoreType.DMA((3,)),
            pltpu.SemaphoreType.DMA((3,)),
        ],
        compiler_params=pltpu.CompilerParams(
            collective_id=0, has_side_effects=True, vmem_limit_bytes=63 * 1024 * 1024
        ),
        name="monarch",
    )(tokens, cotangent, up_first, up_second, down_first, down_second)
    return pl.pallas_call(
        write_out,
        out_shape=shapes,
        in_specs=[in_vmem] * 6,
        out_specs=[in_hbm] * 6,
        scratch_shapes=[pltpu.SemaphoreType.DMA((6,))],
        name="write_out",
    )(*results)


def solution(mesh):
    placed = (
        P("dp", "tensor"),
        P("dp", "tensor"),
        P("tensor", None, None),
        P("tensor", None, None),
        P("tensor", None, None),
        P("tensor", None, None),
    )
    return jax.shard_map(
        local,
        mesh=mesh,
        in_specs=placed,
        out_specs=(
            P("dp", "tensor"),
            P("dp", "tensor"),
            P("tensor", "dp", None),
            P("tensor", "dp", None),
            P("tensor", "dp", None),
            P("tensor", "dp", None),
        ),
        check_vma=False,
    )
```

```python
import functools

import jax
import jax.numpy as jnp
from jax import lax
from jax.experimental import pallas as pl
from jax.experimental.pallas import tpu as pltpu
from jax.sharding import PartitionSpec as P

MESH = pl.DeviceIdType.MESH
F32 = jnp.float32
BF16 = jnp.bfloat16
LANES = 128
ROWS = 16


def dot(left, right, left_dim, right_dim):
    return lax.dot_general(
        left, right, (((left_dim,), (right_dim,)), ((), ())), preferred_element_type=F32
    )


def kernel(
    sizes, factor,
    x_hbm, g_hbm, u1_hbm, u2_hbm, d1_hbm, d2_hbm,
    out_hbm, gt_hbm, gu1_hbm, gu2_hbm, gd1_hbm, gd2_hbm,
    x, g, u1, u2, d1, d2, out, gt, gsum,
    send, recv, wide, nk, bk, hid, slope, gpre,
    home, part, packed, landed, direct, half, half_packed, half_landed,
    in_sem, out_sem, send_sem, recv_sem, psend_sem, precv_sem, hsend_sem, hrecv_sem,
):
    nt, nd, chunks, kd = sizes
    nx = nd // 2
    me = lax.axis_index("tensor")
    my_dp = lax.axis_index("dp")
    my_half = my_dp // nx
    my_x = lax.rem(my_dp, nx)
    other_half = 1 - my_half
    partner = other_half * nx + my_x
    run_half = me // (nt // 2)
    sides = (run_half, 1 - run_half)
    hidden_blocks = nt * kd
    tok = chunks * LANES

    barrier = pltpu.get_barrier_semaphore()
    step = jnp.where(me >= nt // 2, 1, -1)

    def tensor_peer(j):
        return lax.rem(me + nt + step * j, nt)

    def greet_tensor(j):
        peer = tensor_peer(j)
        pl.semaphore_signal(barrier, inc=1, device_id={"tensor": peer}, device_id_type=MESH)

    def x_peer(j):
        return lax.rem(my_x + j, nx)

    for j in range(nx):
        pl.semaphore_signal(
            barrier, inc=1, device_id={"dp": other_half * nx + x_peer(j)}, device_id_type=MESH
        )
    for j in range(1, nt):
        greet_tensor(j)
    for j in range(1, nx):
        pl.semaphore_signal(
            barrier, inc=1, device_id={"dp": my_half * nx + x_peer(j)}, device_id_type=MESH
        )

    loads = [
        pltpu.make_async_copy(src, dst, in_sem.at[i])
        for i, (src, dst) in enumerate(
            ((x_hbm, x), (u1_hbm, u1), (g_hbm, g), (d2_hbm, d2), (u2_hbm, u2), (d1_hbm, d1))
        )
    ]
    for load in loads:
        load.start()

    def exchange(which):
        pltpu.make_async_copy(
            send.at[which, me], recv.at[which, me], recv_sem.at[which]
        ).start()

        def one(j, carry):
            peer = tensor_peer(j)
            side = lax.rem(peer // (nt // 2) + run_half, 2) if which == 3 else 0
            pltpu.make_async_remote_copy(
                src_ref=send.at[which, peer],
                dst_ref=recv.at[which, me],
                send_sem=send_sem.at[which],
                recv_sem=recv_sem.at[which + side],
                device_id={"tensor": peer},
                device_id_type=MESH,
            ).start()
            return carry

        lax.fori_loop(1, nt, one, 0)

    def arrived(which):
        pltpu.make_async_copy(recv.at[which], recv.at[which], recv_sem.at[which]).wait()

    def narrow_to_send(which, weight, rows):
        for tc in range(chunks):
            wide[which % 2, pl.ds(tc, hidden_blocks, stride=chunks), :] = dot(
                weight[0], rows[tc * LANES:(tc + 1) * LANES, :], 1, 1
            )
        send[which] = wide[which % 2].astype(BF16).reshape(nt, ROWS, LANES)

    def share(which):
        packed[which] = part[which].astype(BF16)
        for j in range(1, nx):
            pltpu.make_async_remote_copy(
                src_ref=packed.at[which, :, x_peer(j)],
                dst_ref=landed.at[which, my_x],
                send_sem=psend_sem.at[which],
                recv_sem=precv_sem.at[which],
                device_id={"dp": my_half * nx + x_peer(j)},
                device_id_type=MESH,
            ).start()

    def hand_over(which):
        others = landed.at[which, pl.ds(0, nx - 1)]
        pltpu.make_async_copy(others, others, precv_sem.at[which]).wait()

        def total(side):
            value = part[which, side, my_x]
            for j in range(1, nx):
                value = value + landed[which, x_peer(j), side].astype(F32)
            return value

        half_packed[which] = total(other_half).astype(BF16)
        across(which).start()
        half[which] = total(my_half)

    def across(which):
        return pltpu.make_async_remote_copy(
            src_ref=half_packed.at[which],
            dst_ref=half_landed.at[which],
            send_sem=hsend_sem.at[which],
            recv_sem=hrecv_sem.at[which],
            device_id={"dp": partner},
            device_id_type=MESH,
        )

    def finish(which):
        across(which).wait_recv()
        gsum[which] = (half[which] + half_landed[which].astype(F32)) * factor

    def finish_direct():
        others = direct.at[pl.ds(0, nd - 1)]
        pltpu.make_async_copy(others, others, precv_sem.at[3]).wait()
        value = part[3, my_half, my_x]
        for j in range(1, nd):
            value = value + direct[lax.rem(my_dp + j, nd)].astype(F32)
        gsum[3] = value * factor

    stores = []

    def store(src, dst):
        copy = pltpu.make_async_copy(src, dst, out_sem.at[len(stores)])
        copy.start()
        stores.append(copy)

    def store_sum(which, target):
        for k in range(kd):
            store(gsum.at[which, pl.ds(k * share_rows, share_rows)], target.at[k])

    loads[0].wait()
    loads[1].wait()
    narrow_to_send(0, u1, x)
    pl.semaphore_wait(barrier, nt - 1 + nd - 1)
    exchange(0)
    loads[2].wait()
    loads[3].wait()
    narrow_to_send(1, d2, g)
    exchange(1)
    loads[4].wait()
    loads[5].wait()

    arrived(0)
    wide[0] = recv[0].reshape(nt * ROWS, LANES).astype(F32)
    for k in range(kd):
        for tc in range(chunks):
            nk[k, :, tc * LANES:(tc + 1) * LANES] = wide[
                0, pl.ds(k * chunks + tc, nt, stride=ROWS), :
            ].astype(BF16)
        preact = dot(u2[k], nk[k], 0, 0)
        sigma = 1.0 / (1.0 + jnp.exp(-preact))
        hidden = (preact * sigma).astype(BF16)
        hid[k] = hidden
        slope[k] = sigma * (1.0 + preact * (1.0 - sigma))
        mixed = dot(d1[k], hidden, 1, 0)
        for tc in range(chunks):
            wide[1, pl.ds(k * chunks + tc, nt, stride=ROWS), :] = mixed[
                :, tc * LANES:(tc + 1) * LANES
            ]
    send[2] = wide[1].astype(BF16).reshape(nt, ROWS, LANES)
    exchange(2)

    arrived(1)
    wide[0] = recv[1].reshape(nt * ROWS, LANES).astype(F32)
    for k in range(kd):
        for tc in range(chunks):
            bk[k, :, tc * LANES:(tc + 1) * LANES] = wide[
                0, pl.ds(k * chunks + tc, nt, stride=ROWS), :
            ].astype(BF16)
        grad_pre = (dot(d1[k], bk[k], 0, 0) * slope[k]).astype(BF16)
        gpre[k] = grad_pre
        back = dot(u2[k], grad_pre, 1, 0)
        for tc in range(chunks):
            wide[1, pl.ds(k * chunks + tc, nt, stride=ROWS), :] = back[
                :, tc * LANES:(tc + 1) * LANES
            ]
    send[3] = wide[1].astype(BF16).reshape(nt, ROWS, LANES)
    exchange(3)

    share_rows = nt // nd
    for k in range(kd):
        part[1, :, :, k * share_rows:(k + 1) * share_rows, :] = dot(bk[k], hid[k], 1, 1).reshape(
            2, nx, share_rows, LANES
        )
    share(1)
    for k in range(kd):
        part[0, :, :, k * share_rows:(k + 1) * share_rows, :] = dot(nk[k], gpre[k], 1, 1).reshape(
            2, nx, share_rows, LANES
        )
    share(0)

    def unpack(which):
        wide[which % 2] = recv[which].reshape(nt * ROWS, LANES).astype(F32)
        for tc in range(chunks):
            home[which % 2, tc] = wide[
                which % 2, pl.ds(tc, hidden_blocks, stride=chunks), :
            ].astype(BF16)

    def factor_grad(which, other):
        grad = jnp.zeros((hidden_blocks, LANES), F32)
        for tc in range(chunks):
            grad = grad + dot(home[which % 2, tc], other[tc * LANES:(tc + 1) * LANES, :], 1, 0)
        part[which] = grad.reshape(2, nx, hidden_blocks // nd, LANES)

    def leave(which, weight, residual, result):
        for tc in range(chunks):
            span = slice(tc * LANES, (tc + 1) * LANES)
            result[span, :] = (
                residual[span, :].astype(F32) + dot(home[which % 2, tc], weight[0], 0, 0)
            ).astype(BF16)

    def arrived_side(side):
        block = recv.at[3, pl.ds(sides[side] * (nt // 2), nt // 2)]
        pltpu.make_async_copy(block, block, recv_sem.at[3 + side]).wait()

    def unpack_side(side):
        count = nt * ROWS // 2
        block = recv[3, pl.ds(sides[side] * (nt // 2), nt // 2)]
        wide[1, side * count:(side + 1) * count, :] = block.reshape(count, LANES).astype(F32)
        for tc in range(chunks):
            home[1, tc, side_rows(side), :] = wide[
                1, pl.ds(side * count + tc, hidden_blocks // 2, stride=chunks), :
            ].astype(BF16)

    def side_rows(side):
        return slice(side * hidden_blocks // 2, (side + 1) * hidden_blocks // 2)

    def share_side(side):
        target = sides[side]
        grad = jnp.zeros((hidden_blocks // 2, LANES), F32)
        for tc in range(chunks):
            span = slice(tc * LANES, (tc + 1) * LANES)
            grad = grad + dot(home[1, tc, side_rows(side), :], x[span, :], 1, 0)
        grad = grad.reshape(nx, hidden_blocks // nd, LANES)
        part[3, target] = grad
        packed[3, target] = grad.astype(BF16)
        for j in range(nx):
            copy = pltpu.make_async_remote_copy(
                src_ref=packed.at[3, target, x_peer(j)],
                dst_ref=direct.at[my_dp],
                send_sem=psend_sem.at[3],
                recv_sem=precv_sem.at[3],
                device_id={"dp": target * nx + x_peer(j)},
                device_id_type=MESH,
            )
            if j > 0:
                copy.start()
            else:
                pl.when(target != my_half)(copy.start)

    arrived(2)
    unpack(2)
    factor_grad(2, g)
    share(2)
    leave(2, d2, x, out)
    store(out, out_hbm)

    for side in range(2):
        arrived_side(side)
        unpack_side(side)
        share_side(side)
    hand_over(1)
    hand_over(0)
    hand_over(2)
    for tc in range(chunks):
        span = slice(tc * LANES, (tc + 1) * LANES)
        value = g[span, :].astype(F32)
        for side in range(2):
            rows = pl.ds(sides[side] * (hidden_blocks // 2), hidden_blocks // 2)
            value = value + dot(home[1, tc, side_rows(side), :], u1[0, rows, :], 0, 0)
        gt[span, :] = value.astype(BF16)
    store(gt, gt_hbm)
    finish(1)
    store_sum(1, gd1_hbm)
    finish(0)
    store_sum(0, gu2_hbm)
    finish(2)
    store(gsum.at[2], gd2_hbm.at[0])
    finish_direct()
    store(gsum.at[3], gu1_hbm.at[0])

    for which in range(4):
        sent = send.at[which, pl.ds(0, nt - 1)]
        pltpu.make_async_copy(sent, sent, send_sem.at[which]).wait()
    for which in range(3):
        sent = packed.at[which, :, pl.ds(0, nx - 1)]
        pltpu.make_async_copy(sent, sent, psend_sem.at[which]).wait()
        across(which).wait_send()
    sent = direct.at[pl.ds(0, nd - 1)]
    pltpu.make_async_copy(sent, sent, psend_sem.at[3]).wait()
    for copy in stores:
        copy.wait()


def write_out(*refs):
    count = len(refs) // 2
    sems = refs[-1]
    copies = [
        pltpu.make_async_copy(refs[i], refs[count + i], sems.at[i]) for i in range(count)
    ]
    for copy in copies:
        copy.start()
    for copy in copies:
        copy.wait()


def local(tokens, cotangent, up_first, up_second, down_first, down_second):
    nt, nd = lax.axis_size("tensor"), lax.axis_size("dp")
    tok, width = tokens.shape
    kd, blocks, _ = up_second.shape
    hidden_blocks = up_first.shape[1]
    chunks = tok // LANES
    slab = hidden_blocks // nd
    factor = float(tok * nd) ** -0.5
    shapes = (
        jax.ShapeDtypeStruct(tokens.shape, BF16),
        jax.ShapeDtypeStruct(tokens.shape, BF16),
        jax.ShapeDtypeStruct((1, slab, width), F32),
        jax.ShapeDtypeStruct((kd, blocks // nd, LANES), F32),
        jax.ShapeDtypeStruct((kd, blocks // nd, LANES), F32),
        jax.ShapeDtypeStruct((1, slab, width), F32),
    )
    in_vmem = pl.BlockSpec(memory_space=pltpu.VMEM)
    in_hbm = pl.BlockSpec(memory_space=pltpu.HBM)
    results = pl.pallas_call(
        functools.partial(kernel, (nt, nd, chunks, kd), factor),
        out_shape=shapes,
        in_specs=[in_hbm] * 6,
        out_specs=[in_hbm] * 6,
        scratch_shapes=[
            pltpu.VMEM(tokens.shape, BF16),
            pltpu.VMEM(tokens.shape, BF16),
            pltpu.VMEM(up_first.shape, BF16),
            pltpu.VMEM(up_second.shape, BF16),
            pltpu.VMEM(down_first.shape, BF16),
            pltpu.VMEM(down_second.shape, BF16),
            pltpu.VMEM(tokens.shape, BF16),
            pltpu.VMEM(tokens.shape, BF16),
            pltpu.VMEM((4, slab, LANES), F32),
            pltpu.VMEM((4, nt, ROWS, LANES), BF16),
            pltpu.VMEM((4, nt, ROWS, LANES), BF16),
            pltpu.VMEM((2, nt * ROWS, LANES), F32),
            pltpu.VMEM((kd, blocks, tok), BF16),
            pltpu.VMEM((kd, blocks, tok), BF16),
            pltpu.VMEM((kd, LANES, tok), BF16),
            pltpu.VMEM((kd, LANES, tok), F32),
            pltpu.VMEM((kd, LANES, tok), BF16),
            pltpu.VMEM((2, chunks, hidden_blocks, LANES), BF16),
            pltpu.VMEM((4, 2, nd // 2, slab, LANES), F32),
            pltpu.VMEM((4, 2, nd // 2, slab, LANES), BF16),
            pltpu.VMEM((3, nd // 2, 2, slab, LANES), BF16),
            pltpu.VMEM((nd, slab, LANES), BF16),
            pltpu.VMEM((3, slab, LANES), F32),
            pltpu.VMEM((3, slab, LANES), BF16),
            pltpu.VMEM((3, slab, LANES), BF16),
            pltpu.SemaphoreType.DMA((6,)),
            pltpu.SemaphoreType.DMA((4 + 2 * kd,)),
            pltpu.SemaphoreType.DMA((4,)),
            pltpu.SemaphoreType.DMA((5,)),
            pltpu.SemaphoreType.DMA((4,)),
            pltpu.SemaphoreType.DMA((4,)),
            pltpu.SemaphoreType.DMA((3,)),
            pltpu.SemaphoreType.DMA((3,)),
        ],
        compiler_params=pltpu.CompilerParams(
            collective_id=0, has_side_effects=True, vmem_limit_bytes=63 * 1024 * 1024
        ),
        name="monarch",
    )(tokens, cotangent, up_first, up_second, down_first, down_second)
    return pl.pallas_call(
        write_out,
        out_shape=shapes,
        in_specs=[in_vmem] * 6,
        out_specs=[in_hbm] * 6,
        scratch_shapes=[pltpu.SemaphoreType.DMA((6,))],
        name="write_out",
    )(*results)


def solution(mesh):
    placed = (
        P("dp", "tensor"),
        P("dp", "tensor"),
        P("tensor", None, None),
        P("tensor", None, None),
        P("tensor", None, None),
        P("tensor", None, None),
    )
    return jax.shard_map(
        local,
        mesh=mesh,
        in_specs=placed,
        out_specs=(
            P("dp", "tensor"),
            P("dp", "tensor"),
            P("tensor", "dp", None),
            P("tensor", "dp", None),
            P("tensor", "dp", None),
            P("tensor", "dp", None),
        ),
        check_vma=False,
    )
```

```python
import functools

import jax
import jax.numpy as jnp
from jax import lax
from jax.experimental import pallas as pl
from jax.experimental.pallas import tpu as pltpu
from jax.sharding import PartitionSpec as P

MESH = pl.DeviceIdType.MESH
F32 = jnp.float32
BF16 = jnp.bfloat16
LANES = 128
ROWS = 16


def dot(left, right, left_dim, right_dim):
    return lax.dot_general(
        left, right, (((left_dim,), (right_dim,)), ((), ())), preferred_element_type=F32
    )


def kernel(
    sizes, factor,
    x_hbm, g_hbm, u1_hbm, u2_hbm, d1_hbm, d2_hbm,
    out_hbm, gt_hbm, gu1_hbm, gu2_hbm, gd1_hbm, gd2_hbm,
    x, g, u1, u2, d1, d2, out, gt, gsum,
    send, recv, wide, nk, bk, hid, slope, gpre,
    home, part, packed, landed, direct, half, half_packed, half_landed,
    in_sem, out_sem, send_sem, recv_sem, psend_sem, precv_sem, hsend_sem, hrecv_sem,
):
    nt, nd, chunks, kd = sizes
    nx = nd // 2
    me = lax.axis_index("tensor")
    my_dp = lax.axis_index("dp")
    my_half = my_dp // nx
    my_x = lax.rem(my_dp, nx)
    other_half = 1 - my_half
    partner = other_half * nx + my_x
    run_half = me // (nt // 2)
    sides = (run_half, 1 - run_half)
    hidden_blocks = nt * kd
    tok = chunks * LANES

    barrier = pltpu.get_barrier_semaphore()
    step = jnp.where(me >= nt // 2, 1, -1)

    def tensor_peer(j):
        return lax.rem(me + nt + step * j, nt)

    def greet_tensor(j):
        peer = tensor_peer(j)
        pl.semaphore_signal(barrier, inc=1, device_id={"tensor": peer}, device_id_type=MESH)

    def x_peer(j):
        return lax.rem(my_x + j, nx)

    for j in range(nx):
        pl.semaphore_signal(
            barrier, inc=1, device_id={"dp": other_half * nx + x_peer(j)}, device_id_type=MESH
        )
    for j in range(1, nt):
        greet_tensor(j)
    for j in range(1, nx):
        pl.semaphore_signal(
            barrier, inc=1, device_id={"dp": my_half * nx + x_peer(j)}, device_id_type=MESH
        )

    loads = [
        pltpu.make_async_copy(src, dst, in_sem.at[i])
        for i, (src, dst) in enumerate(
            ((x_hbm, x), (u1_hbm, u1), (g_hbm, g), (d2_hbm, d2), (u2_hbm, u2), (d1_hbm, d1))
        )
    ]
    for load in loads:
        load.start()

    def exchange(which):
        pltpu.make_async_copy(
            send.at[which, me], recv.at[which, me], recv_sem.at[which]
        ).start()

        def one(j, carry):
            peer = lax.rem(me + j, nt) if which == 3 else tensor_peer(j)
            side = lax.rem(peer // (nt // 2) + run_half, 2) if which == 3 else 0
            pltpu.make_async_remote_copy(
                src_ref=send.at[which, peer],
                dst_ref=recv.at[which, me],
                send_sem=send_sem.at[which],
                recv_sem=recv_sem.at[which + side],
                device_id={"tensor": peer},
                device_id_type=MESH,
            ).start()
            return carry

        lax.fori_loop(1, nt, one, 0)

    def arrived(which):
        pltpu.make_async_copy(recv.at[which], recv.at[which], recv_sem.at[which]).wait()

    def narrow_to_send(which, weight, rows):
        for tc in range(chunks):
            wide[which % 2, pl.ds(tc, hidden_blocks, stride=chunks), :] = dot(
                weight[0], rows[tc * LANES:(tc + 1) * LANES, :], 1, 1
            )
        send[which] = wide[which % 2].astype(BF16).reshape(nt, ROWS, LANES)

    def share(which):
        packed[which] = part[which].astype(BF16)
        for j in range(1, nx):
            pltpu.make_async_remote_copy(
                src_ref=packed.at[which, :, x_peer(j)],
                dst_ref=landed.at[which, my_x],
                send_sem=psend_sem.at[which],
                recv_sem=precv_sem.at[which],
                device_id={"dp": my_half * nx + x_peer(j)},
                device_id_type=MESH,
            ).start()

    def hand_over(which):
        others = landed.at[which, pl.ds(0, nx - 1)]
        pltpu.make_async_copy(others, others, precv_sem.at[which]).wait()

        def total(side):
            value = part[which, side, my_x]
            for j in range(1, nx):
                value = value + landed[which, x_peer(j), side].astype(F32)
            return value

        half_packed[which] = total(other_half).astype(BF16)
        across(which).start()
        half[which] = total(my_half)

    def across(which):
        return pltpu.make_async_remote_copy(
            src_ref=half_packed.at[which],
            dst_ref=half_landed.at[which],
            send_sem=hsend_sem.at[which],
            recv_sem=hrecv_sem.at[which],
            device_id={"dp": partner},
            device_id_type=MESH,
        )

    def finish(which):
        across(which).wait_recv()
        gsum[which] = (half[which] + half_landed[which].astype(F32)) * factor

    def finish_direct():
        others = direct.at[pl.ds(0, nd - 1)]
        pltpu.make_async_copy(others, others, precv_sem.at[3]).wait()
        value = part[3, my_half, my_x]
        for j in range(1, nd):
            value = value + direct[lax.rem(my_dp + j, nd)].astype(F32)
        gsum[3] = value * factor

    stores = []

    def store(src, dst):
        copy = pltpu.make_async_copy(src, dst, out_sem.at[len(stores)])
        copy.start()
        stores.append(copy)

    def store_sum(which, target):
        for k in range(kd):
            store(gsum.at[which, pl.ds(k * share_rows, share_rows)], target.at[k])

    loads[0].wait()
    loads[1].wait()
    narrow_to_send(0, u1, x)
    pl.semaphore_wait(barrier, nt - 1 + nd - 1)
    exchange(0)
    loads[2].wait()
    loads[3].wait()
    narrow_to_send(1, d2, g)
    exchange(1)
    loads[4].wait()
    loads[5].wait()

    arrived(0)
    wide[0] = recv[0].reshape(nt * ROWS, LANES).astype(F32)
    for k in range(kd):
        for tc in range(chunks):
            nk[k, :, tc * LANES:(tc + 1) * LANES] = wide[
                0, pl.ds(k * chunks + tc, nt, stride=ROWS), :
            ].astype(BF16)
        preact = dot(u2[k], nk[k], 0, 0)
        sigma = 1.0 / (1.0 + jnp.exp(-preact))
        hidden = (preact * sigma).astype(BF16)
        hid[k] = hidden
        slope[k] = sigma * (1.0 + preact * (1.0 - sigma))
        mixed = dot(d1[k], hidden, 1, 0)
        for tc in range(chunks):
            wide[1, pl.ds(k * chunks + tc, nt, stride=ROWS), :] = mixed[
                :, tc * LANES:(tc + 1) * LANES
            ]
    send[2] = wide[1].astype(BF16).reshape(nt, ROWS, LANES)
    exchange(2)

    arrived(1)
    wide[0] = recv[1].reshape(nt * ROWS, LANES).astype(F32)
    for k in range(kd):
        for tc in range(chunks):
            bk[k, :, tc * LANES:(tc + 1) * LANES] = wide[
                0, pl.ds(k * chunks + tc, nt, stride=ROWS), :
            ].astype(BF16)
        grad_pre = (dot(d1[k], bk[k], 0, 0) * slope[k]).astype(BF16)
        gpre[k] = grad_pre
        back = dot(u2[k], grad_pre, 1, 0)
        for tc in range(chunks):
            wide[1, pl.ds(k * chunks + tc, nt, stride=ROWS), :] = back[
                :, tc * LANES:(tc + 1) * LANES
            ]
    send[3] = wide[1].astype(BF16).reshape(nt, ROWS, LANES)
    exchange(3)

    share_rows = nt // nd
    for k in range(kd):
        part[1, :, :, k * share_rows:(k + 1) * share_rows, :] = dot(bk[k], hid[k], 1, 1).reshape(
            2, nx, share_rows, LANES
        )
    share(1)
    for k in range(kd):
        part[0, :, :, k * share_rows:(k + 1) * share_rows, :] = dot(nk[k], gpre[k], 1, 1).reshape(
            2, nx, share_rows, LANES
        )
    share(0)

    def unpack(which):
        wide[which % 2] = recv[which].reshape(nt * ROWS, LANES).astype(F32)
        for tc in range(chunks):
            home[which % 2, tc] = wide[
                which % 2, pl.ds(tc, hidden_blocks, stride=chunks), :
            ].astype(BF16)

    def factor_grad(which, other):
        grad = jnp.zeros((hidden_blocks, LANES), F32)
        for tc in range(chunks):
            grad = grad + dot(home[which % 2, tc], other[tc * LANES:(tc + 1) * LANES, :], 1, 0)
        part[which] = grad.reshape(2, nx, hidden_blocks // nd, LANES)

    def leave(which, weight, residual, result):
        for tc in range(chunks):
            span = slice(tc * LANES, (tc + 1) * LANES)
            result[span, :] = (
                residual[span, :].astype(F32) + dot(home[which % 2, tc], weight[0], 0, 0)
            ).astype(BF16)

    def arrived_side(side):
        block = recv.at[3, pl.ds(sides[side] * (nt // 2), nt // 2)]
        pltpu.make_async_copy(block, block, recv_sem.at[3 + side]).wait()

    def unpack_side(side):
        count = nt * ROWS // 2
        block = recv[3, pl.ds(sides[side] * (nt // 2), nt // 2)]
        wide[1, side * count:(side + 1) * count, :] = block.reshape(count, LANES).astype(F32)
        for tc in range(chunks):
            home[1, tc, side_rows(side), :] = wide[
                1, pl.ds(side * count + tc, hidden_blocks // 2, stride=chunks), :
            ].astype(BF16)

    def side_rows(side):
        return slice(side * hidden_blocks // 2, (side + 1) * hidden_blocks // 2)

    def share_side(side):
        target = sides[side]
        grad = jnp.zeros((hidden_blocks // 2, LANES), F32)
        for tc in range(chunks):
            span = slice(tc * LANES, (tc + 1) * LANES)
            grad = grad + dot(home[1, tc, side_rows(side), :], x[span, :], 1, 0)
        grad = grad.reshape(nx, hidden_blocks // nd, LANES)
        part[3, target] = grad
        packed[3, target] = grad.astype(BF16)
        for j in range(nx):
            copy = pltpu.make_async_remote_copy(
                src_ref=packed.at[3, target, x_peer(j)],
                dst_ref=direct.at[my_dp],
                send_sem=psend_sem.at[3],
                recv_sem=precv_sem.at[3],
                device_id={"dp": target * nx + x_peer(j)},
                device_id_type=MESH,
            )
            if j > 0:
                copy.start()
            else:
                pl.when(target != my_half)(copy.start)

    arrived(2)
    unpack(2)
    factor_grad(2, g)
    share(2)
    leave(2, d2, x, out)
    store(out, out_hbm)

    for side in range(2):
        arrived_side(side)
        unpack_side(side)
        share_side(side)
    hand_over(1)
    hand_over(0)
    hand_over(2)
    for tc in range(chunks):
        span = slice(tc * LANES, (tc + 1) * LANES)
        value = g[span, :].astype(F32)
        for side in range(2):
            rows = pl.ds(sides[side] * (hidden_blocks // 2), hidden_blocks // 2)
            value = value + dot(home[1, tc, side_rows(side), :], u1[0, rows, :], 0, 0)
        gt[span, :] = value.astype(BF16)
    store(gt, gt_hbm)
    finish(1)
    store_sum(1, gd1_hbm)
    finish(0)
    store_sum(0, gu2_hbm)
    finish(2)
    store(gsum.at[2], gd2_hbm.at[0])
    finish_direct()
    store(gsum.at[3], gu1_hbm.at[0])

    for which in range(4):
        sent = send.at[which, pl.ds(0, nt - 1)]
        pltpu.make_async_copy(sent, sent, send_sem.at[which]).wait()
    for which in range(3):
        sent = packed.at[which, :, pl.ds(0, nx - 1)]
        pltpu.make_async_copy(sent, sent, psend_sem.at[which]).wait()
        across(which).wait_send()
    sent = direct.at[pl.ds(0, nd - 1)]
    pltpu.make_async_copy(sent, sent, psend_sem.at[3]).wait()
    for copy in stores:
        copy.wait()


def write_out(*refs):
    count = len(refs) // 2
    sems = refs[-1]
    copies = [
        pltpu.make_async_copy(refs[i], refs[count + i], sems.at[i]) for i in range(count)
    ]
    for copy in copies:
        copy.start()
    for copy in copies:
        copy.wait()


def local(tokens, cotangent, up_first, up_second, down_first, down_second):
    nt, nd = lax.axis_size("tensor"), lax.axis_size("dp")
    tok, width = tokens.shape
    kd, blocks, _ = up_second.shape
    hidden_blocks = up_first.shape[1]
    chunks = tok // LANES
    slab = hidden_blocks // nd
    factor = float(tok * nd) ** -0.5
    shapes = (
        jax.ShapeDtypeStruct(tokens.shape, BF16),
        jax.ShapeDtypeStruct(tokens.shape, BF16),
        jax.ShapeDtypeStruct((1, slab, width), F32),
        jax.ShapeDtypeStruct((kd, blocks // nd, LANES), F32),
        jax.ShapeDtypeStruct((kd, blocks // nd, LANES), F32),
        jax.ShapeDtypeStruct((1, slab, width), F32),
    )
    in_vmem = pl.BlockSpec(memory_space=pltpu.VMEM)
    in_hbm = pl.BlockSpec(memory_space=pltpu.HBM)
    results = pl.pallas_call(
        functools.partial(kernel, (nt, nd, chunks, kd), factor),
        out_shape=shapes,
        in_specs=[in_hbm] * 6,
        out_specs=[in_hbm] * 6,
        scratch_shapes=[
            pltpu.VMEM(tokens.shape, BF16),
            pltpu.VMEM(tokens.shape, BF16),
            pltpu.VMEM(up_first.shape, BF16),
            pltpu.VMEM(up_second.shape, BF16),
            pltpu.VMEM(down_first.shape, BF16),
            pltpu.VMEM(down_second.shape, BF16),
            pltpu.VMEM(tokens.shape, BF16),
            pltpu.VMEM(tokens.shape, BF16),
            pltpu.VMEM((4, slab, LANES), F32),
            pltpu.VMEM((4, nt, ROWS, LANES), BF16),
            pltpu.VMEM((4, nt, ROWS, LANES), BF16),
            pltpu.VMEM((2, nt * ROWS, LANES), F32),
            pltpu.VMEM((kd, blocks, tok), BF16),
            pltpu.VMEM((kd, blocks, tok), BF16),
            pltpu.VMEM((kd, LANES, tok), BF16),
            pltpu.VMEM((kd, LANES, tok), F32),
            pltpu.VMEM((kd, LANES, tok), BF16),
            pltpu.VMEM((2, chunks, hidden_blocks, LANES), BF16),
            pltpu.VMEM((4, 2, nd // 2, slab, LANES), F32),
            pltpu.VMEM((4, 2, nd // 2, slab, LANES), BF16),
            pltpu.VMEM((3, nd // 2, 2, slab, LANES), BF16),
            pltpu.VMEM((nd, slab, LANES), BF16),
            pltpu.VMEM((3, slab, LANES), F32),
            pltpu.VMEM((3, slab, LANES), BF16),
            pltpu.VMEM((3, slab, LANES), BF16),
            pltpu.SemaphoreType.DMA((6,)),
            pltpu.SemaphoreType.DMA((4 + 2 * kd,)),
            pltpu.SemaphoreType.DMA((4,)),
            pltpu.SemaphoreType.DMA((5,)),
            pltpu.SemaphoreType.DMA((4,)),
            pltpu.SemaphoreType.DMA((4,)),
            pltpu.SemaphoreType.DMA((3,)),
            pltpu.SemaphoreType.DMA((3,)),
        ],
        compiler_params=pltpu.CompilerParams(
            collective_id=0, has_side_effects=True, vmem_limit_bytes=63 * 1024 * 1024
        ),
        name="monarch",
    )(tokens, cotangent, up_first, up_second, down_first, down_second)
    return pl.pallas_call(
        write_out,
        out_shape=shapes,
        in_specs=[in_vmem] * 6,
        out_specs=[in_hbm] * 6,
        scratch_shapes=[pltpu.SemaphoreType.DMA((6,))],
        name="write_out",
    )(*results)


def solution(mesh):
    placed = (
        P("dp", "tensor"),
        P("dp", "tensor"),
        P("tensor", None, None),
        P("tensor", None, None),
        P("tensor", None, None),
        P("tensor", None, None),
    )
    return jax.shard_map(
        local,
        mesh=mesh,
        in_specs=placed,
        out_specs=(
            P("dp", "tensor"),
            P("dp", "tensor"),
            P("tensor", "dp", None),
            P("tensor", "dp", None),
            P("tensor", "dp", None),
            P("tensor", "dp", None),
        ),
        check_vma=False,
    )
```

```python
import functools

import jax
import jax.numpy as jnp
from jax import lax
from jax.experimental import pallas as pl
from jax.experimental.pallas import tpu as pltpu
from jax.sharding import PartitionSpec as P

MESH = pl.DeviceIdType.MESH
F32 = jnp.float32
BF16 = jnp.bfloat16
LANES = 128
ROWS = 16


def dot(left, right, left_dim, right_dim):
    return lax.dot_general(
        left, right, (((left_dim,), (right_dim,)), ((), ())), preferred_element_type=F32
    )


def kernel(
    sizes, factor,
    x_hbm, g_hbm, u1_hbm, u2_hbm, d1_hbm, d2_hbm,
    out_hbm, gt_hbm, gu1_hbm, gu2_hbm, gd1_hbm, gd2_hbm,
    x, g, u1, u2, d1, d2, out, gt, gsum,
    send, recv, wide, nk, bk, hid, slope, gpre,
    home, part, packed, landed, direct, half, half_packed, half_landed,
    in_sem, out_sem, send_sem, recv_sem, psend_sem, precv_sem, hsend_sem, hrecv_sem, ready,
):
    nt, nd, chunks, kd = sizes
    nx = nd // 2
    me = lax.axis_index("tensor")
    my_dp = lax.axis_index("dp")
    my_half = my_dp // nx
    my_x = lax.rem(my_dp, nx)
    other_half = 1 - my_half
    partner = other_half * nx + my_x
    run_half = me // (nt // 2)
    sides = (run_half, 1 - run_half)
    hidden_blocks = nt * kd
    tok = chunks * LANES

    loads = [
        pltpu.make_async_copy(src, dst, in_sem.at[i])
        for i, (src, dst) in enumerate(
            ((x_hbm, x), (u1_hbm, u1), (g_hbm, g), (d2_hbm, d2), (u2_hbm, u2), (d1_hbm, d1))
        )
    ]
    for load in loads:
        load.start()

    barrier = pltpu.get_barrier_semaphore()
    step = jnp.where(me >= nt // 2, 1, -1)

    def tensor_peer(j):
        return lax.rem(me + nt + step * j, nt)

    def greet_tensor(j):
        peer = tensor_peer(j)
        pl.semaphore_signal(barrier, inc=1, device_id={"tensor": peer}, device_id_type=MESH)

    def x_peer(j):
        return lax.rem(my_x + j, nx)

    def tell_other_half(semaphore):
        for j in range(nx):
            pl.semaphore_signal(
                semaphore,
                inc=1,
                device_id={"dp": other_half * nx + x_peer(j)},
                device_id_type=MESH,
            )

    pl.when(my_half == 1)(lambda: tell_other_half(barrier))
    for j in range(1, nt):
        greet_tensor(j)
    for j in range(1, nx):
        pl.semaphore_signal(
            barrier, inc=1, device_id={"dp": my_half * nx + x_peer(j)}, device_id_type=MESH
        )


    def exchange(which):
        pltpu.make_async_copy(
            send.at[which, me], recv.at[which, me], recv_sem.at[which]
        ).start()

        def one(j, carry):
            peer = lax.rem(me + j, nt) if which == 3 else tensor_peer(j)
            side = lax.rem(peer // (nt // 2) + run_half, 2) if which == 3 else 0
            pltpu.make_async_remote_copy(
                src_ref=send.at[which, peer],
                dst_ref=recv.at[which, me],
                send_sem=send_sem.at[which],
                recv_sem=recv_sem.at[which + side],
                device_id={"tensor": peer},
                device_id_type=MESH,
            ).start()
            return carry

        lax.fori_loop(1, nt, one, 0)

    def arrived(which):
        pltpu.make_async_copy(recv.at[which], recv.at[which], recv_sem.at[which]).wait()

    def narrow_to_send(which, weight, rows):
        for tc in range(chunks):
            wide[which % 2, pl.ds(tc, hidden_blocks, stride=chunks), :] = dot(
                weight[0], rows[tc * LANES:(tc + 1) * LANES, :], 1, 1
            )
        send[which] = wide[which % 2].astype(BF16).reshape(nt, ROWS, LANES)

    def share(which):
        packed[which] = part[which].astype(BF16)
        for j in range(1, nx):
            pltpu.make_async_remote_copy(
                src_ref=packed.at[which, :, x_peer(j)],
                dst_ref=landed.at[which, my_x],
                send_sem=psend_sem.at[which],
                recv_sem=precv_sem.at[which],
                device_id={"dp": my_half * nx + x_peer(j)},
                device_id_type=MESH,
            ).start()

    def hand_over(which):
        others = landed.at[which, pl.ds(0, nx - 1)]
        pltpu.make_async_copy(others, others, precv_sem.at[which]).wait()

        def total(side):
            value = part[which, side, my_x]
            for j in range(1, nx):
                value = value + landed[which, x_peer(j), side].astype(F32)
            return value

        half_packed[which] = total(other_half).astype(BF16)
        across(which).start()
        half[which] = total(my_half)

    def across(which):
        return pltpu.make_async_remote_copy(
            src_ref=half_packed.at[which],
            dst_ref=half_landed.at[which],
            send_sem=hsend_sem.at[which],
            recv_sem=hrecv_sem.at[which],
            device_id={"dp": partner},
            device_id_type=MESH,
        )

    def finish(which):
        across(which).wait_recv()
        gsum[which] = (half[which] + half_landed[which].astype(F32)) * factor

    def finish_direct():
        others = direct.at[pl.ds(0, nd - 1)]
        pltpu.make_async_copy(others, others, precv_sem.at[3]).wait()
        value = part[3, my_half, my_x]
        for j in range(1, nd):
            value = value + direct[lax.rem(my_dp + j, nd)].astype(F32)
        gsum[3] = value * factor

    stores = []

    def store(src, dst):
        copy = pltpu.make_async_copy(src, dst, out_sem.at[len(stores)])
        copy.start()
        stores.append(copy)

    def store_sum(which, target):
        for k in range(kd):
            store(gsum.at[which, pl.ds(k * share_rows, share_rows)], target.at[k])

    loads[0].wait()
    loads[1].wait()
    narrow_to_send(0, u1, x)
    pl.semaphore_wait(barrier, nt - 1 + nx - 1 + other_half * nx)
    pl.when(my_half == 0)(lambda: tell_other_half(ready))
    exchange(0)
    loads[2].wait()
    loads[3].wait()
    narrow_to_send(1, d2, g)
    exchange(1)
    loads[4].wait()
    loads[5].wait()

    arrived(0)
    wide[0] = recv[0].reshape(nt * ROWS, LANES).astype(F32)
    for k in range(kd):
        for tc in range(chunks):
            nk[k, :, tc * LANES:(tc + 1) * LANES] = wide[
                0, pl.ds(k * chunks + tc, nt, stride=ROWS), :
            ].astype(BF16)
        preact = dot(u2[k], nk[k], 0, 0)
        sigma = 1.0 / (1.0 + jnp.exp(-preact))
        hidden = (preact * sigma).astype(BF16)
        hid[k] = hidden
        slope[k] = sigma * (1.0 + preact * (1.0 - sigma))
        mixed = dot(d1[k], hidden, 1, 0)
        for tc in range(chunks):
            wide[1, pl.ds(k * chunks + tc, nt, stride=ROWS), :] = mixed[
                :, tc * LANES:(tc + 1) * LANES
            ]
    send[2] = wide[1].astype(BF16).reshape(nt, ROWS, LANES)
    exchange(2)

    arrived(1)
    wide[0] = recv[1].reshape(nt * ROWS, LANES).astype(F32)
    for k in range(kd):
        for tc in range(chunks):
            bk[k, :, tc * LANES:(tc + 1) * LANES] = wide[
                0, pl.ds(k * chunks + tc, nt, stride=ROWS), :
            ].astype(BF16)
        grad_pre = (dot(d1[k], bk[k], 0, 0) * slope[k]).astype(BF16)
        gpre[k] = grad_pre
        back = dot(u2[k], grad_pre, 1, 0)
        for tc in range(chunks):
            wide[1, pl.ds(k * chunks + tc, nt, stride=ROWS), :] = back[
                :, tc * LANES:(tc + 1) * LANES
            ]
    send[3] = wide[1].astype(BF16).reshape(nt, ROWS, LANES)
    exchange(3)

    share_rows = nt // nd
    for k in range(kd):
        part[1, :, :, k * share_rows:(k + 1) * share_rows, :] = dot(bk[k], hid[k], 1, 1).reshape(
            2, nx, share_rows, LANES
        )
    share(1)
    for k in range(kd):
        part[0, :, :, k * share_rows:(k + 1) * share_rows, :] = dot(nk[k], gpre[k], 1, 1).reshape(
            2, nx, share_rows, LANES
        )
    share(0)

    def unpack(which):
        wide[which % 2] = recv[which].reshape(nt * ROWS, LANES).astype(F32)
        for tc in range(chunks):
            home[which % 2, tc] = wide[
                which % 2, pl.ds(tc, hidden_blocks, stride=chunks), :
            ].astype(BF16)

    def factor_grad(which, other):
        grad = jnp.zeros((hidden_blocks, LANES), F32)
        for tc in range(chunks):
            grad = grad + dot(home[which % 2, tc], other[tc * LANES:(tc + 1) * LANES, :], 1, 0)
        part[which] = grad.reshape(2, nx, hidden_blocks // nd, LANES)

    def leave(which, weight, residual, result):
        for tc in range(chunks):
            span = slice(tc * LANES, (tc + 1) * LANES)
            result[span, :] = (
                residual[span, :].astype(F32) + dot(home[which % 2, tc], weight[0], 0, 0)
            ).astype(BF16)

    def arrived_side(side):
        block = recv.at[3, pl.ds(sides[side] * (nt // 2), nt // 2)]
        pltpu.make_async_copy(block, block, recv_sem.at[3 + side]).wait()

    def unpack_side(side):
        count = nt * ROWS // 2
        block = recv[3, pl.ds(sides[side] * (nt // 2), nt // 2)]
        wide[1, side * count:(side + 1) * count, :] = block.reshape(count, LANES).astype(F32)
        for tc in range(chunks):
            home[1, tc, side_rows(side), :] = wide[
                1, pl.ds(side * count + tc, hidden_blocks // 2, stride=chunks), :
            ].astype(BF16)

    def side_rows(side):
        return slice(side * hidden_blocks // 2, (side + 1) * hidden_blocks // 2)

    def share_side(side):
        target = sides[side]
        grad = jnp.zeros((hidden_blocks // 2, LANES), F32)
        for tc in range(chunks):
            span = slice(tc * LANES, (tc + 1) * LANES)
            grad = grad + dot(home[1, tc, side_rows(side), :], x[span, :], 1, 0)
        grad = grad.reshape(nx, hidden_blocks // nd, LANES)
        part[3, target] = grad
        packed[3, target] = grad.astype(BF16)
        for j in range(nx):
            copy = pltpu.make_async_remote_copy(
                src_ref=packed.at[3, target, x_peer(j)],
                dst_ref=direct.at[my_dp],
                send_sem=psend_sem.at[3],
                recv_sem=precv_sem.at[3],
                device_id={"dp": target * nx + x_peer(j)},
                device_id_type=MESH,
            )
            if j > 0:
                copy.start()
            else:
                pl.when(target != my_half)(copy.start)

    arrived(2)
    unpack(2)
    factor_grad(2, g)
    share(2)
    leave(2, d2, x, out)
    store(out, out_hbm)

    pl.when(my_half == 1)(lambda: pl.semaphore_wait(ready, nx))
    for side in range(2):
        arrived_side(side)
        unpack_side(side)
        share_side(side)
    hand_over(1)
    hand_over(0)
    hand_over(2)
    for tc in range(chunks):
        span = slice(tc * LANES, (tc + 1) * LANES)
        value = g[span, :].astype(F32)
        for side in range(2):
            rows = pl.ds(sides[side] * (hidden_blocks // 2), hidden_blocks // 2)
            value = value + dot(home[1, tc, side_rows(side), :], u1[0, rows, :], 0, 0)
        gt[span, :] = value.astype(BF16)
    store(gt, gt_hbm)
    finish(1)
    store_sum(1, gd1_hbm)
    finish(0)
    store_sum(0, gu2_hbm)
    finish(2)
    store(gsum.at[2], gd2_hbm.at[0])
    finish_direct()
    store(gsum.at[3], gu1_hbm.at[0])

    for which in range(4):
        sent = send.at[which, pl.ds(0, nt - 1)]
        pltpu.make_async_copy(sent, sent, send_sem.at[which]).wait()
    for which in range(3):
        sent = packed.at[which, :, pl.ds(0, nx - 1)]
        pltpu.make_async_copy(sent, sent, psend_sem.at[which]).wait()
        across(which).wait_send()
    sent = direct.at[pl.ds(0, nd - 1)]
    pltpu.make_async_copy(sent, sent, psend_sem.at[3]).wait()
    for copy in stores:
        copy.wait()


def write_out(*refs):
    count = len(refs) // 2
    sems = refs[-1]
    copies = [
        pltpu.make_async_copy(refs[i], refs[count + i], sems.at[i]) for i in range(count)
    ]
    for copy in copies:
        copy.start()
    for copy in copies:
        copy.wait()


def local(tokens, cotangent, up_first, up_second, down_first, down_second):
    nt, nd = lax.axis_size("tensor"), lax.axis_size("dp")
    tok, width = tokens.shape
    kd, blocks, _ = up_second.shape
    hidden_blocks = up_first.shape[1]
    chunks = tok // LANES
    slab = hidden_blocks // nd
    factor = float(tok * nd) ** -0.5
    shapes = (
        jax.ShapeDtypeStruct(tokens.shape, BF16),
        jax.ShapeDtypeStruct(tokens.shape, BF16),
        jax.ShapeDtypeStruct((1, slab, width), F32),
        jax.ShapeDtypeStruct((kd, blocks // nd, LANES), F32),
        jax.ShapeDtypeStruct((kd, blocks // nd, LANES), F32),
        jax.ShapeDtypeStruct((1, slab, width), F32),
    )
    in_vmem = pl.BlockSpec(memory_space=pltpu.VMEM)
    in_hbm = pl.BlockSpec(memory_space=pltpu.HBM)
    results = pl.pallas_call(
        functools.partial(kernel, (nt, nd, chunks, kd), factor),
        out_shape=shapes,
        in_specs=[in_hbm] * 6,
        out_specs=[in_hbm] * 6,
        scratch_shapes=[
            pltpu.VMEM(tokens.shape, BF16),
            pltpu.VMEM(tokens.shape, BF16),
            pltpu.VMEM(up_first.shape, BF16),
            pltpu.VMEM(up_second.shape, BF16),
            pltpu.VMEM(down_first.shape, BF16),
            pltpu.VMEM(down_second.shape, BF16),
            pltpu.VMEM(tokens.shape, BF16),
            pltpu.VMEM(tokens.shape, BF16),
            pltpu.VMEM((4, slab, LANES), F32),
            pltpu.VMEM((4, nt, ROWS, LANES), BF16),
            pltpu.VMEM((4, nt, ROWS, LANES), BF16),
            pltpu.VMEM((2, nt * ROWS, LANES), F32),
            pltpu.VMEM((kd, blocks, tok), BF16),
            pltpu.VMEM((kd, blocks, tok), BF16),
            pltpu.VMEM((kd, LANES, tok), BF16),
            pltpu.VMEM((kd, LANES, tok), F32),
            pltpu.VMEM((kd, LANES, tok), BF16),
            pltpu.VMEM((2, chunks, hidden_blocks, LANES), BF16),
            pltpu.VMEM((4, 2, nd // 2, slab, LANES), F32),
            pltpu.VMEM((4, 2, nd // 2, slab, LANES), BF16),
            pltpu.VMEM((3, nd // 2, 2, slab, LANES), BF16),
            pltpu.VMEM((nd, slab, LANES), BF16),
            pltpu.VMEM((3, slab, LANES), F32),
            pltpu.VMEM((3, slab, LANES), BF16),
            pltpu.VMEM((3, slab, LANES), BF16),
            pltpu.SemaphoreType.DMA((6,)),
            pltpu.SemaphoreType.DMA((4 + 2 * kd,)),
            pltpu.SemaphoreType.DMA((4,)),
            pltpu.SemaphoreType.DMA((5,)),
            pltpu.SemaphoreType.DMA((4,)),
            pltpu.SemaphoreType.DMA((4,)),
            pltpu.SemaphoreType.DMA((3,)),
            pltpu.SemaphoreType.DMA((3,)),
            pltpu.SemaphoreType.REGULAR,
        ],
        compiler_params=pltpu.CompilerParams(
            collective_id=0, has_side_effects=True, vmem_limit_bytes=63 * 1024 * 1024
        ),
        name="monarch",
    )(tokens, cotangent, up_first, up_second, down_first, down_second)
    return pl.pallas_call(
        write_out,
        out_shape=shapes,
        in_specs=[in_vmem] * 6,
        out_specs=[in_hbm] * 6,
        scratch_shapes=[pltpu.SemaphoreType.DMA((6,))],
        name="write_out",
    )(*results)


def solution(mesh):
    placed = (
        P("dp", "tensor"),
        P("dp", "tensor"),
        P("tensor", None, None),
        P("tensor", None, None),
        P("tensor", None, None),
        P("tensor", None, None),
    )
    return jax.shard_map(
        local,
        mesh=mesh,
        in_specs=placed,
        out_specs=(
            P("dp", "tensor"),
            P("dp", "tensor"),
            P("tensor", "dp", None),
            P("tensor", "dp", None),
            P("tensor", "dp", None),
            P("tensor", "dp", None),
        ),
        check_vma=False,
    )
```
